512 devices in a mesh: ctx: 64 (over x, z, core), head: 8 (over y).
Axes of the slice: x: 4, y: 8, z: 8, core: 2. Of those that a mesh axis runs over, the one named last changes fastest.
Arguments:
- queries: bfloat16 [8192, 1024], P('ctx', 'head'), may hold values from -200 to 200
- keys: bfloat16 [2, 8192, 128], P(None, 'ctx'), may hold values from -8 to 8
- values: bfloat16 [2, 8192, 128], P(None, 'ctx'), may hold values from -6 to 6
- grad_out: bfloat16 [8192, 1024], P('ctx', 'head'), may hold values from -6 to 6
- episode_lengths: int32 [8], replicated, may hold values from 1 to 4096, 8192 in all
- key_stretches: int32 [128, 4], replicated, may hold values from 0 to 127, as said below
Outputs:
- attn_out: bfloat16 [8192, 1024], P('ctx', 'head')
- grad_queries: bfloat16 [8192, 1024], P('ctx', 'head')
- grad_keys: bfloat16 [2, 8192, 128], P(None, 'ctx')
- grad_values: bfloat16 [2, 8192, 128], P(None, 'ctx')
The draws below stay inside these ranges and needn't reach their ends.
Inputs may be any that keep to these rules, and one draw needn't show every extreme that they name: Row k of key_stretches (device d = k // 2) lists the stretch of row k itself; 2 stretches up to 7 before it, clipped at 0; and one recall entry: the later of the two stretches of device (d + 32) mod (64) that lie before row k's stretch, or row k's own stretch if neither does. Entries may repeat.
All inputs are finite; a program needn't handle non-finite values.
Results may differ from the reference program's by a relative error of at most 0.017.
Values may be sent and summed in bfloat16 or wider, within the bound.
A program may use at most 64 MiB of HBM per device.

```python
import math
import jax
import jax.numpy as jnp
import numpy as np
from jax import lax

HEAD_SIZE = 128
QUERY_HEADS = 8
KEY_VALUE_HEADS = 2
C = 64
SPAN = 8
LIST = 4
NCHUNK = 128
TOKEN_COUNT = 8192
EPIS = 8
MOST_EP = 4096
N_CTX = 64


def base_keys(key):
    return jax.random.normal(jax.random.fold_in(key, 17), (KEY_VALUE_HEADS, TOKEN_COUNT, HEAD_SIZE), jnp.float32)


def draw_keys(key, part):
    shared = base_keys(key)
    return jnp.clip(shared, -8.0, 8.0).astype(jnp.bfloat16)


def draw_queries(key, part):
    key = jax.random.fold_in(key, 3)
    result = jnp.clip(jax.random.normal(key, (TOKEN_COUNT, QUERY_HEADS, HEAD_SIZE), jnp.float32), -6.0, 6.0)
    return result.reshape(TOKEN_COUNT, QUERY_HEADS * HEAD_SIZE).astype(jnp.bfloat16)


def draw_key_stretches(key, part):
    key = jax.random.fold_in(key, 5)
    ctx_count = NCHUNK // 2
    row_ids = jnp.arange(NCHUNK)
    device_row = row_ids // 2
    global_stretch = jnp.where(row_ids % 2 == 0, device_row, NCHUNK - 1 - device_row)
    row_keys = jax.random.split(key, NCHUNK)
    orders = jax.vmap(lambda row_key: jax.random.permutation(row_key, SPAN - 1))(row_keys)
    recent = jnp.maximum(global_stretch[:, None] - (orders[:, :LIST - 2].astype(jnp.int32) + 1), 0)
    partner = (device_row + ctx_count // 2) % ctx_count
    first_cand = jnp.minimum(partner, NCHUNK - 1 - partner)
    second_cand = jnp.maximum(partner, NCHUNK - 1 - partner)
    recall = jnp.where(second_cand < global_stretch, second_cand, jnp.where(first_cand < global_stretch, first_cand, global_stretch))
    return jnp.concatenate([global_stretch[:, None], recent, recall[:, None]], axis=1).astype(jnp.int32)


def shard_levels(own_key, shape, pieces, low, high):
    gain, own = 1.0, jax.random.fold_in(own_key, 6)
    for axis_at, parts in pieces:
        steps = jnp.exp(jax.random.uniform(jax.random.fold_in(own, axis_at), (parts,), jnp.float32, low / len(pieces), high / len(pieces)))
        gain = gain * jnp.repeat(steps, shape[axis_at] // parts).reshape([-1 if axis == axis_at else 1 for axis in range(len(shape))])
    return gain


def length_profile(count, total, bound, slope):
    weights = [(1 << 20) // math.isqrt(standing ** slope) + 1 for standing in range(2, count + 1)]
    surplus, given = total - bound - (count - 1), [1] * (count - 1)
    while surplus > 0:
        free = [i for i in range(count - 1) if given[i] < bound]
        mass, budget = sum([weights[i] for i in free]), surplus
        for i in free:
            addition = min(bound - given[i], max(1, budget * weights[i] // mass), surplus)
            given[i] = given[i] + addition
            surplus = surplus - addition
    return np.array([bound] + given)


def ragged_sizes(own_key, number_of, total, most, skew):
    if number_of == 2:
        one = jax.random.randint(own_key, (), max(1, total - most), min(most, total - 1) + 1)
        return jnp.stack([one, total - one])
    lengths = jnp.asarray(length_profile(number_of, total, most, skew), jnp.int32)
    couples = (number_of - 1) // 2
    source_of, receiver = lengths[1:1 + 2 * couples:2], lengths[2:2 + 2 * couples:2]
    room = jnp.minimum(source_of - 1, most - receiver)
    passed = jax.random.randint(jax.random.fold_in(own_key, 1), (couples,), 0, 1 << 20) % (room + 1)
    lengths = lengths.at[1:1 + 2 * couples:2].set(source_of - passed).at[2:2 + 2 * couples:2].set(receiver + passed)
    return lengths[jax.random.permutation(jax.random.fold_in(own_key, 2), number_of)]


def gaussian(rng, dims, deviation, limit, pieces=(), kind=jnp.bfloat16):
    drawn = deviation * jax.random.normal(rng, dims, jnp.float32)
    if pieces:
        drawn = drawn * shard_levels(rng, dims, pieces, -0.22, 0.18)
    return jnp.clip(drawn, -limit, limit).astype(kind)


def setup_inputs(seed: int = 0) -> dict:
    splits = jax.random.split(jax.random.key(seed), 7)
    return {
        "queries": draw_queries(jax.random.fold_in(splits[6], 71), 0),
        "keys": draw_keys(jax.random.fold_in(splits[6], 71), 0),
        "values": gaussian(splits[2], (KEY_VALUE_HEADS, TOKEN_COUNT, HEAD_SIZE), 1.0, 6.0, ((1, 64),)),
        "grad_out": gaussian(splits[3], (TOKEN_COUNT, QUERY_HEADS * HEAD_SIZE), 1.0, 6.0, ((0, 64), (1, 8))),
        "episode_lengths": ragged_sizes(splits[4], EPIS, TOKEN_COUNT, MOST_EP, 2).astype(jnp.int32),
        "key_stretches": draw_key_stretches(jax.random.fold_in(splits[6], 71), 0),
    }


mask_floor = -1e+30

def row_positions(row_ids, stretch_rows, stretch_total):
    array_stretch = row_ids // stretch_rows
    device_row = array_stretch // 2
    global_stretch = jnp.where(array_stretch % 2 == 0, device_row, stretch_total - 1 - device_row)
    return (global_stretch * stretch_rows + row_ids % stretch_rows).astype(jnp.int32)

def episode_of(positions, episode_ends):
    return lax.optimization_barrier(jnp.sum((episode_ends[None, :] <= positions[:, None]).astype(jnp.int32), axis=1))

def reference(queries, keys, values, grad_out, episode_lengths, key_stretches):
    stretch_total = 2 * N_CTX
    inv_scale = 1.0 / math.sqrt(HEAD_SIZE)
    row_ids = jnp.arange(TOKEN_COUNT, dtype=jnp.int32)
    positions = row_positions(row_ids, C, stretch_total)
    episode_ends = jnp.cumsum(episode_lengths).astype(jnp.int32)
    episodes = episode_of(positions, episode_ends)
    stretch_ids = jnp.arange(stretch_total, dtype=jnp.int32)
    listed_table = jnp.any(key_stretches[:, :, None] == stretch_ids[None, None, :], axis=1)
    key_listed = jnp.take(listed_table, positions // C, axis=1)
    block_rows = math.gcd(TOKEN_COUNT, 512)
    block_count = TOKEN_COUNT // block_rows
    heads_per_group = QUERY_HEADS // KEY_VALUE_HEADS
    query_heads = queries.reshape(TOKEN_COUNT, QUERY_HEADS, HEAD_SIZE)
    grad_heads = grad_out.reshape(TOKEN_COUNT, QUERY_HEADS, HEAD_SIZE)
    outputs = []
    query_grads = []
    key_gradient_rows = [jnp.zeros((TOKEN_COUNT, HEAD_SIZE), jnp.float32) for key_value_slot in range(KEY_VALUE_HEADS)]
    value_gradient_rows = [jnp.zeros((TOKEN_COUNT, HEAD_SIZE), jnp.float32) for key_value_slot in range(KEY_VALUE_HEADS)]
    for head_index in range(QUERY_HEADS):
        key_value_group = head_index // heads_per_group
        head_keys = keys[key_value_group]
        head_values = values[key_value_group]
        head_queries = query_heads[:, head_index]
        head_grads = grad_heads[:, head_index]

        def one_block(totals, block_index):
            first_row = block_index * block_rows
            block_pos = lax.dynamic_slice_in_dim(positions, first_row, block_rows, 0)
            block_eps = lax.dynamic_slice_in_dim(episodes, first_row, block_rows, 0)
            block_ids = first_row + jnp.arange(block_rows, dtype=jnp.int32)
            visible = (positions[None, :] <= block_pos[:, None]) & (episodes[None, :] == block_eps[:, None])
            visible = visible & jnp.take(key_listed, block_ids // C, axis=0)
            block_queries = lax.dynamic_slice_in_dim(head_queries, first_row, block_rows, 0)
            block_grads = lax.dynamic_slice_in_dim(head_grads, first_row, block_rows, 0)
            scores = jnp.dot(block_queries, head_keys.T, preferred_element_type=jnp.float32) * inv_scale
            masked = jnp.where(visible, scores, mask_floor)
            row_max = lax.optimization_barrier(jnp.max(masked, axis=1))
            row_sum = lax.optimization_barrier(jnp.sum(jnp.where(visible, jnp.exp(masked - row_max[:, None]), 0.0), axis=1))
            log_total = row_max + jnp.log(row_sum)
            weights = jnp.where(visible, jnp.exp(masked - log_total[:, None]), 0.0)
            rounded = weights.astype(jnp.bfloat16)
            output = jnp.dot(rounded, head_values, preferred_element_type=jnp.float32)
            inner = lax.optimization_barrier(jnp.sum(block_grads.astype(jnp.float32) * output, axis=1))
            grad_weights = jnp.dot(block_grads, head_values.T, preferred_element_type=jnp.float32)
            grad_scores = (weights * (grad_weights - inner[:, None])).astype(jnp.bfloat16)
            query_grad = jnp.dot(grad_scores, head_keys, preferred_element_type=jnp.float32) * inv_scale
            key_total = totals[0] + jnp.dot(grad_scores.T, block_queries, preferred_element_type=jnp.float32) * inv_scale
            value_total = totals[1] + jnp.dot(rounded.T, block_grads, preferred_element_type=jnp.float32)
            return ((key_total, value_total), (output.astype(jnp.bfloat16), query_grad.astype(jnp.bfloat16)))
        start_totals = (jnp.zeros((TOKEN_COUNT, HEAD_SIZE), jnp.float32), jnp.zeros((TOKEN_COUNT, HEAD_SIZE), jnp.float32))
        totals, blocks_out = lax.scan(one_block, start_totals, jnp.arange(block_count, dtype=jnp.int32))
        key_gradient_rows[key_value_group] = key_gradient_rows[key_value_group] + totals[0]
        value_gradient_rows[key_value_group] = value_gradient_rows[key_value_group] + totals[1]
        outputs.append(blocks_out[0].reshape(TOKEN_COUNT, HEAD_SIZE))
        query_grads.append(blocks_out[1].reshape(TOKEN_COUNT, HEAD_SIZE))
    attn_out = jnp.stack(outputs, axis=1).reshape(TOKEN_COUNT, QUERY_HEADS * HEAD_SIZE)
    grad_queries = jnp.stack(query_grads, axis=1).reshape(TOKEN_COUNT, QUERY_HEADS * HEAD_SIZE)
    grad_keys = jnp.stack(key_gradient_rows, axis=0).astype(jnp.bfloat16)
    grad_values = jnp.stack(value_gradient_rows, axis=0).astype(jnp.bfloat16)
    return (attn_out, grad_queries, grad_keys, grad_values)
```

```python
import functools
import math

import jax
import jax.numpy as jnp
from jax import lax
from jax.experimental import pallas as pl
from jax.experimental.pallas import tpu as pltpu
from jax.sharding import PartitionSpec as P

MESH = pl.DeviceIdType.MESH
C = 64
QUARTER = 16
HEADS = 8
GROUP = 4
PAIRS = 64
CHIPS = 32
SLOTS = 11
OWN, OTHER, RECALL = 7, 8, 9
D = 128
MASKED = -1e30
EVEN_STEPS = (1, 2, 3)
ODD_STEPS = (1, 2, 3, 4)
INV = 1.0 / math.sqrt(D)


def device_of(pair):
    pair = lax.rem(pair + 2 * PAIRS, PAIRS)
    return jnp.where(pair < PAIRS // 2, 2 * pair, 2 * PAIRS - 1 - 2 * pair)


def attend_kernel(
    q_hbm, k_hbm, v_hbm, do_hbm, ep_hbm, ks_hbm,
    rows_out, sums_out,
    q_ref, do_ref, kv_ref, bias_ref, part_ref, back_ref, rows_ref, quarter_ref, heads_ref,
    ep_ref, ks_ref,
    in_sems, kv_sem, q_sem, back_sem, rows_sem, heads_sem, sums_sem,
    kv_send, q_send, back_send, rows_send, heads_send, sums_send,
):
    d = lax.axis_index("ctx")
    h = lax.axis_index("head")
    m, c = d // 2, d % 2
    g, j = h // GROUP, h % GROUP
    mine = jnp.where(c == 0, m, PAIRS - 1 - m)
    other = PAIRS - 1 - mine
    other_core = 2 * m + 1 - c
    far_chip = lax.rem(m + CHIPS // 2, CHIPS)
    late = jnp.where(m >= CHIPS // 2, 1, 0)

    even_to = [device_of(mine + k) for k in EVEN_STEPS]
    even_from = [device_of(mine - k) for k in EVEN_STEPS]
    odd_with = [device_of(other + k) for k in ODD_STEPS]
    far = [2 * far_chip, 2 * far_chip + 1]
    heads = [(h + k) % HEADS for k in range(1, HEADS)]
    group_heads = [g * GROUP + (j + k) % GROUP for k in range(1, GROUP)]

    barrier = pltpu.get_barrier_semaphore()

    def greet(ctx_at, head_at):
        pl.semaphore_signal(barrier, inc=1, device_id=(ctx_at, head_at), device_id_type=MESH)

    for at in even_to + even_from + [other_core] + far:
        greet(at, h)
    for at in odd_with:
        pl.when(at != d)(functools.partial(greet, at, h))
    for at in heads:
        greet(d, at)

    even_rows, odd_rows = pl.ds(c * C, C), pl.ds((1 - c) * C, C)
    loads = [
        pltpu.make_async_copy(ep_hbm, ep_ref, in_sems.at[0]),
        pltpu.make_async_copy(ks_hbm, ks_ref, in_sems.at[1]),
    ]
    own_q = [
        pltpu.make_async_copy(q_hbm.at[even_rows], q_ref.at[0], in_sems.at[2]),
        pltpu.make_async_copy(do_hbm.at[even_rows], do_ref.at[0], in_sems.at[3]),
    ]
    own_kv = [
        pltpu.make_async_copy(k_hbm.at[g, even_rows], kv_ref.at[OWN, 0], kv_sem),
        pltpu.make_async_copy(v_hbm.at[g, even_rows], kv_ref.at[OWN, 1], kv_sem),
    ]
    for copy in loads + own_q + own_kv:
        copy.start()

    self_count = jnp.where(lax.rem(mine, PAIRS // 2) < 2, 1, 0)
    pl.semaphore_wait(barrier, 6 + 4 + 1 + 2 + 7 - self_count)

    kv_sends, kv_maybe = [], []

    def send_kv(rows, slot, at, may_be_self=False):
        for which, ref in enumerate((k_hbm, v_hbm)):
            remote = pltpu.make_async_remote_copy(
                src_ref=ref.at[g, rows], dst_ref=kv_ref.at[slot, which], send_sem=kv_send, recv_sem=kv_sem,
                device_id=(at, h), device_id_type=MESH,
            )
            if may_be_self:
                local = pltpu.make_async_copy(ref.at[g, rows], kv_ref.at[slot, which], kv_sem)
                pl.when(at != d)(remote.start)
                pl.when(at == d)(local.start)
                kv_maybe.append((at, remote))
            else:
                remote.start()
                kv_sends.append(remote)

    for k, at in zip(ODD_STEPS[::-1], odd_with[::-1]):
        send_kv(odd_rows, 8 - 2 * k, at, may_be_self=True)
    for k, at in zip(EVEN_STEPS[::-1], even_to[::-1]):
        send_kv(even_rows, 7 - 2 * k, at)
    far_rows = pl.ds(late * C, C)
    for at in far:
        send_kv(far_rows, RECALL + c, at)
    send_kv(odd_rows, OTHER, other_core)
    q_sends = [
        pltpu.make_async_remote_copy(
            src_ref=ref.at[odd_rows], dst_ref=to.at[1], send_sem=q_send.at[n], recv_sem=q_sem.at[n],
            device_id=(other_core, h), device_id_type=MESH,
        )
        for n, (ref, to) in enumerate(((q_hbm, q_ref), (do_hbm, do_ref)))
    ]
    for copy in q_sends:
        copy.start()

    for copy in loads:
        copy.wait()
    lane = lax.broadcasted_iota(jnp.int32, (1, 2 * C), 1)
    query_pos = 2 * mine * C + lane
    first_pos = jnp.zeros_like(query_pos)
    start = jnp.int32(0)
    for e in range(HEADS - 1):
        start = start + ep_ref[e]
        first_pos = jnp.where(start <= query_pos, start, first_pos)
    row_of = (2 * d + c, 2 * other_core + c)
    entries = [[ks_ref[e, row] for e in range(4)] for row in row_of]
    far_valid = jnp.logical_or(late == 1, c == 1)
    key_row = lax.broadcasted_iota(jnp.int32, (C, 2 * C), 0)
    for slot in range(SLOTS):
        if slot < RECALL:
            stretch = 2 * mine - 7 + slot
        else:
            at = far[slot - RECALL]
            stretch = jnp.where(far_valid, jnp.where(late == 1, at, 2 * PAIRS - 1 - at), -1)
        base = []
        for row in entries:
            hit = row[0] == stretch
            for entry in row[1:]:
                hit = jnp.logical_or(hit, entry == stretch)
            base.append(jnp.where(hit, stretch * C, -(1 << 20)))
        key_pos = key_row + jnp.where(lane < C, base[0], base[1])
        seen = (key_pos >= first_pos) & (key_pos <= query_pos)
        bias_ref[pl.ds(slot * C, C), :] = jnp.where(seen, 0.0, MASKED)

    for copy in own_q:
        copy.wait()
    for copy in q_sends:
        copy.wait_recv()
    pltpu.make_async_copy(kv_ref, kv_ref, kv_sem).wait()

    queries = q_ref[...].reshape(2 * C, D)
    grads = do_ref[...].reshape(2 * C, D)
    keys = kv_ref[:, 0].reshape(SLOTS * C, D)
    values = kv_ref[:, 1].reshape(SLOTS * C, D)
    last = (((1,), (1,)), ((), ()))
    first = (((0,), (0,)), ((), ()))
    plain = (((1,), (0,)), ((), ()))

    def dot(a, b, dims):
        return lax.dot_general(a, b, dims, preferred_element_type=jnp.float32)

    scores = dot(keys, queries, last) * INV + bias_ref[...]
    top = jnp.max(scores, axis=0, keepdims=True)
    weights = jnp.exp(scores - top)
    weights = weights * (1.0 / jnp.sum(weights, axis=0, keepdims=True))
    grad_weights = dot(values, grads, last)
    inner = jnp.sum(weights * grad_weights, axis=0, keepdims=True)
    rounded = weights.astype(jnp.bfloat16)
    grad_scores = (weights * (grad_weights - inner)).astype(jnp.bfloat16)
    part_ref[:, 0] = (dot(grad_scores, queries, plain) * INV).astype(jnp.bfloat16).reshape(SLOTS, C, D)
    part_ref[:, 1] = dot(rounded, grads, plain).astype(jnp.bfloat16).reshape(SLOTS, C, D)

    back_sends, back_maybe = [], []

    def send_back(slot, to, at, may_be_self=False):
        remote = pltpu.make_async_remote_copy(
            src_ref=part_ref.at[slot], dst_ref=back_ref.at[to], send_sem=back_send, recv_sem=back_sem,
            device_id=(at, h), device_id_type=MESH,
        )
        if may_be_self:
            local = pltpu.make_async_copy(part_ref.at[slot], back_ref.at[to], back_sem)
            pl.when(at != d)(remote.start)
            pl.when(at == d)(local.start)
            back_maybe.append((at, remote))
        else:
            remote.start()
            back_sends.append(remote)

    for k, at in zip(ODD_STEPS[::-1], odd_with[::-1]):
        send_back(8 - 2 * k, k - 1, at, may_be_self=True)
    for k, at in zip(EVEN_STEPS[::-1], even_from[::-1]):
        send_back(7 - 2 * k, 4 + k, at)
    for n, at in enumerate(far):
        send_back(RECALL + n, 8 + c, at)
    send_back(OTHER, 4, other_core)

    out = dot(rounded, values, first)
    grad_queries = dot(grad_scores, keys, first) * INV
    rows_ref[0] = out.astype(jnp.bfloat16)
    rows_ref[1] = grad_queries.astype(jnp.bfloat16)
    rows_copies = [
        pltpu.make_async_copy(rows_ref.at[n, pl.ds(0, C)], rows_out.at[n, even_rows], in_sems.at[n])
        for n in range(2)
    ]
    rows_sends = [
        pltpu.make_async_remote_copy(
            src_ref=rows_ref.at[n, pl.ds(C, C)], dst_ref=rows_out.at[n, even_rows],
            send_sem=rows_send.at[n], recv_sem=rows_sem.at[n],
            device_id=(other_core, h), device_id_type=MESH,
        )
        for n in range(2)
    ]
    for copy in rows_copies + rows_sends:
        copy.start()

    pltpu.make_async_copy(back_ref, back_ref, back_sem).wait()

    def read(n):
        return back_ref[n].astype(jnp.float32)

    recalled = read(8) + read(9)
    to_even = jnp.where(late == c, 1.0, 0.0)
    even_total = part_ref[OWN].astype(jnp.float32) + read(5) + read(6) + read(7) + recalled * to_even
    odd_total = read(4) + read(0) + read(1) + read(2) + read(3) + recalled * (1.0 - to_even)
    for q in range(GROUP):
        rows = slice(q * QUARTER, (q + 1) * QUARTER)
        quarter_ref[q, c] = even_total[:, rows].astype(jnp.bfloat16)
        quarter_ref[q, 1 - c] = odd_total[:, rows].astype(jnp.bfloat16)
    head_sends = [
        pltpu.make_async_remote_copy(
            src_ref=quarter_ref.at[at % GROUP], dst_ref=heads_ref.at[k], send_sem=heads_send, recv_sem=heads_sem,
            device_id=(d, at), device_id_type=MESH,
        )
        for k, at in enumerate(group_heads)
    ]
    for copy in head_sends:
        copy.start()
    total = quarter_ref[j].astype(jnp.float32)
    pltpu.make_async_copy(heads_ref, heads_ref, heads_sem).wait()
    for k in range(GROUP - 1):
        total = total + heads_ref[k].astype(jnp.float32)
    sums_out[h] = total.astype(jnp.bfloat16)
    sum_sends = [
        pltpu.make_async_remote_copy(
            src_ref=sums_out.at[h], dst_ref=sums_out.at[h], send_sem=sums_send.at[k], recv_sem=sums_sem.at[k],
            device_id=(d, at), device_id_type=MESH,
        )
        for k, at in enumerate(heads)
    ]
    for copy in sum_sends:
        copy.start()

    for copy in rows_copies:
        copy.wait()
    for copy in rows_sends:
        copy.wait_send()
        copy.wait_recv()
    for copy in q_sends + kv_sends + back_sends + head_sends:
        copy.wait_send()
    for at, copy in kv_maybe + back_maybe:
        pl.when(at != d)(copy.wait_send)
    for copy in sum_sends:
        copy.wait_send()
        copy.wait_recv()


def lay_out_kernel(rows_ref, sums_ref, out_ref, dq_ref, dk_ref, dv_ref):
    out_ref[...] = rows_ref[0]
    dq_ref[...] = rows_ref[1]
    for h in range(HEADS):
        g, q = divmod(h, GROUP)
        for s in range(2):
            rows = slice(s * C + q * QUARTER, s * C + (q + 1) * QUARTER)
            dk_ref[g, rows] = sums_ref[h, s, 0]
            dv_ref[g, rows] = sums_ref[h, s, 1]


def on_device(queries, keys, values, grad_out, episode_lengths, key_stretches):
    vmem = pl.BlockSpec(memory_space=pltpu.VMEM)
    dma = pltpu.SemaphoreType.DMA
    bf16 = jnp.bfloat16
    inputs = [
        pltpu.with_memory_space_constraint(x, pltpu.HBM)
        for x in (queries, keys, values, grad_out, episode_lengths, key_stretches.T)
    ]
    rows, sums = pl.pallas_call(
        attend_kernel,
        out_shape=(
            pltpu.VMEM((2, 2 * C, D), bf16),
            pltpu.VMEM((HEADS, 2, 2, QUARTER, D), bf16),
        ),
        in_specs=[pl.BlockSpec(memory_space=pltpu.HBM)] * 6,
        out_specs=(vmem, vmem),
        scratch_shapes=[
            pltpu.VMEM((2, C, D), bf16),
            pltpu.VMEM((2, C, D), bf16),
            pltpu.VMEM((SLOTS, 2, C, D), bf16),
            pltpu.VMEM((SLOTS * C, 2 * C), jnp.float32),
            pltpu.VMEM((SLOTS, 2, C, D), bf16),
            pltpu.VMEM((SLOTS - 1, 2, C, D), bf16),
            pltpu.VMEM((2, 2 * C, D), bf16),
            pltpu.VMEM((GROUP, 2, 2, QUARTER, D), bf16),
            pltpu.VMEM((GROUP - 1, 2, 2, QUARTER, D), bf16),
            pltpu.SMEM((HEADS,), jnp.int32),
            pltpu.SMEM((4, 2 * PAIRS), jnp.int32),
            dma((4,)), dma, dma((2,)), dma, dma((2,)), dma, dma((HEADS - 1,)),
            dma, dma((2,)), dma, dma((2,)), dma, dma((HEADS - 1,)),
        ],
        compiler_params=pltpu.CompilerParams(
            collective_id=0, has_side_effects=True, vmem_limit_bytes=16 * 1024 * 1024
        ),
        name="attend",
    )(*inputs)
    half = jax.ShapeDtypeStruct((2 * C, D), bf16)
    both = jax.ShapeDtypeStruct((2, 2 * C, D), bf16)
    return pl.pallas_call(
        lay_out_kernel,
        out_shape=(half, half, both, both),
        in_specs=[vmem] * 2,
        out_specs=(vmem,) * 4,
        name="lay_out",
    )(*(pltpu.with_memory_space_constraint(x, pltpu.VMEM) for x in (rows, sums)))


def solution(mesh):
    return jax.shard_map(
        on_device,
        mesh=mesh,
        in_specs=(
            P("ctx", "head"),
            P(None, "ctx", None),
            P(None, "ctx", None),
            P("ctx", "head"),
            P(),
            P(),
        ),
        out_specs=(P("ctx", "head"), P("ctx", "head"), P(None, "ctx", None), P(None, "ctx", None)),
        check_vma=False,
    )
```

```python
import functools
import math

import jax
import jax.numpy as jnp
from jax import lax
from jax.experimental import pallas as pl
from jax.experimental.pallas import tpu as pltpu
from jax.sharding import PartitionSpec as P

MESH = pl.DeviceIdType.MESH
C = 64
HALF = 32
QUARTER = 16
HEADS = 8
GROUP = 4
PAIR = 2
PAIRS = 64
ROWS = PAIR * 2 * C
CHIPS = 32
SLOTS = 11
OWN, OTHER, RECALL = 7, 8, 9
D = 128
MASKED = -1e30
EVEN_STEPS = (1, 2, 3)
ODD_STEPS = (1, 2, 3, 4)
INV = 1.0 / math.sqrt(D)


def device_of(pair):
    pair = lax.rem(pair + 2 * PAIRS, PAIRS)
    return jnp.where(pair < PAIRS // 2, 2 * pair, 2 * PAIRS - 1 - 2 * pair)


def attend_kernel(
    q_hbm, k_hbm, v_hbm, do_hbm, ep_hbm, ks_hbm,
    rows_out, sums_out,
    qdo_ref, kv_ref, bias_ref, stat_ref, part_ref, back_ref, rows_ref, got_ref,
    ep_ref, ks_ref,
    in_sems, kv_sem, q_sem, stat_sem, back_sem, rows_sem, sums_sem,
    kv_send, q_send, stat_send, back_send, rows_send, sums_send,
):
    d = lax.axis_index("ctx")
    h = lax.axis_index("head")
    m, c = d // 2, d % 2
    g, p, b = h // GROUP, h // PAIR % 2, h % PAIR
    mate = h + 1 - 2 * b
    across = h + 2 - 4 * p
    mine = jnp.where(c == 0, m, PAIRS - 1 - m)
    other = PAIRS - 1 - mine
    other_core = 2 * m + 1 - c
    far_chip = lax.rem(m + CHIPS // 2, CHIPS)
    late = jnp.where(m >= CHIPS // 2, 1, 0)

    even_to = [device_of(mine + k) for k in EVEN_STEPS]
    even_from = [device_of(mine - k) for k in EVEN_STEPS]
    odd_with = [device_of(other + k) for k in ODD_STEPS]
    far = [2 * far_chip, 2 * far_chip + 1]
    heads = [(h + k) % HEADS for k in (4, 3, 5, 2, 6, 1, 7)]

    barrier = pltpu.get_barrier_semaphore()

    def greet(ctx_at, head_at):
        pl.semaphore_signal(barrier, inc=1, device_id=(ctx_at, head_at), device_id_type=MESH)

    for at in odd_with[::-1]:
        pl.when(at != d)(functools.partial(greet, at, h))
        greet(at, across)
    for at in even_to + even_from + far + [other_core]:
        greet(at, h)
        greet(at, across)
    for at in heads:
        greet(d, at)
    greet(other_core, mate)

    even_rows, odd_rows = pl.ds(c * C, C), pl.ds((1 - c) * C, C)
    loads = [
        pltpu.make_async_copy(ep_hbm, ep_ref, in_sems.at[0]),
        pltpu.make_async_copy(ks_hbm, ks_ref, in_sems.at[1]),
    ]
    own = [
        pltpu.make_async_copy(q_hbm.at[even_rows], qdo_ref.at[0, b, 0], q_sem),
        pltpu.make_async_copy(do_hbm.at[even_rows], qdo_ref.at[1, b, 0], q_sem),
        pltpu.make_async_copy(k_hbm.at[g, pl.ds(c * C + b * HALF, HALF)], kv_ref.at[OWN, 0], kv_sem),
        pltpu.make_async_copy(v_hbm.at[g, pl.ds(c * C + b * HALF, HALF)], kv_ref.at[OWN, 1], kv_sem),
    ]
    for copy in loads + own:
        copy.start()

    self_count = jnp.where(lax.rem(mine, PAIRS // 2) < 2, 1, 0)
    pl.semaphore_wait(barrier, 2 * (6 + 4 + 1 + 2) + 7 + 1 - self_count)

    sent, sent_maybe = [], []

    def send_kv(stretch, slot, at, may_be_self=False):
        rows = pl.ds(stretch * C + b * HALF, HALF)
        for which, ref in enumerate((k_hbm, v_hbm)):
            remote = pltpu.make_async_remote_copy(
                src_ref=ref.at[g, rows], dst_ref=kv_ref.at[slot, which], send_sem=kv_send, recv_sem=kv_sem,
                device_id=(at, h), device_id_type=MESH,
            )
            if may_be_self:
                local = pltpu.make_async_copy(ref.at[g, rows], kv_ref.at[slot, which], kv_sem)
                pl.when(at != d)(remote.start)
                pl.when(at == d)(local.start)
                sent_maybe.append((at, remote))
            else:
                remote.start()
                sent.append(remote)

    def send_q(rows, which, to):
        for n, ref in enumerate((q_hbm, do_hbm)):
            remote = pltpu.make_async_remote_copy(
                src_ref=ref.at[rows], dst_ref=qdo_ref.at[n, b, which], send_sem=q_send, recv_sem=q_sem,
                device_id=to, device_id_type=MESH,
            )
            remote.start()
            sent.append(remote)

    for k, at in zip(ODD_STEPS[::-1], odd_with[::-1]):
        send_kv(1 - c, 8 - 2 * k, at, may_be_self=True)
    send_q(even_rows, 0, (d, mate))
    send_q(odd_rows, 1, (other_core, mate))
    for k, at in zip(EVEN_STEPS[::-1], even_to[::-1]):
        send_kv(c, 7 - 2 * k, at)
    for at in far:
        send_kv(late, RECALL + c, at)
    send_kv(1 - c, OTHER, other_core)
    send_q(odd_rows, 1, (other_core, h))

    for copy in loads:
        copy.wait()
    lane = lax.broadcasted_iota(jnp.int32, (1, 2 * C), 1)
    query_pos = 2 * mine * C + lane
    first_pos = jnp.zeros_like(query_pos)
    start = jnp.int32(0)
    for e in range(HEADS - 1):
        start = start + ep_ref[e]
        first_pos = jnp.where(start <= query_pos, start, first_pos)
    row_of = (2 * d + c, 2 * other_core + c)
    entries = [[ks_ref[e, row] for e in range(4)] for row in row_of]
    far_valid = jnp.logical_or(late == 1, c == 1)
    key_row = lax.broadcasted_iota(jnp.int32, (HALF, 2 * C), 0) + b * HALF
    for slot in range(SLOTS):
        if slot < RECALL:
            stretch = 2 * mine - 7 + slot
        else:
            at = far[slot - RECALL]
            stretch = jnp.where(far_valid, jnp.where(late == 1, at, 2 * PAIRS - 1 - at), -1)
        base = []
        for row in entries:
            hit = row[0] == stretch
            for entry in row[1:]:
                hit = jnp.logical_or(hit, entry == stretch)
            base.append(jnp.where(hit, stretch * C, -(1 << 20)))
        key_pos = key_row + jnp.where(lane < C, base[0], base[1])
        seen = (key_pos >= first_pos) & (key_pos <= query_pos)
        bias_ref[pl.ds(slot * HALF, HALF), :] = jnp.where(seen, 0.0, MASKED)

    pltpu.make_async_copy(qdo_ref, qdo_ref, q_sem).wait()
    pltpu.make_async_copy(kv_ref, kv_ref, kv_sem).wait()

    queries = qdo_ref[0].reshape(ROWS, D)
    grads = qdo_ref[1].reshape(ROWS, D)
    keys = kv_ref[:, 0].reshape(SLOTS * HALF, D)
    values = kv_ref[:, 1].reshape(SLOTS * HALF, D)
    last = (((1,), (1,)), ((), ()))
    first = (((0,), (0,)), ((), ()))
    plain = (((1,), (0,)), ((), ()))

    def dot(a, b, dims):
        return lax.dot_general(a, b, dims, preferred_element_type=jnp.float32)

    scores = dot(keys, queries, last) * INV + jnp.concatenate([bias_ref[...]] * PAIR, axis=1)
    top = jnp.max(scores, axis=0, keepdims=True)
    weights = jnp.exp(scores - top)
    mass = jnp.sum(weights, axis=0, keepdims=True)
    grad_weights = dot(values, grads, last)
    inner = jnp.sum(weights * grad_weights, axis=0, keepdims=True)

    stat_ref[b, 0:1] = top
    stat_ref[b, 1:2] = mass
    stat_ref[b, 2:3] = inner
    remote = pltpu.make_async_remote_copy(
        src_ref=stat_ref.at[b], dst_ref=stat_ref.at[b], send_sem=stat_send, recv_sem=stat_sem,
        device_id=(d, mate), device_id_type=MESH,
    )
    remote.start()
    sent.append(remote)
    remote.wait_recv()
    tops = [stat_ref[n, 0:1] for n in range(PAIR)]
    top_all = functools.reduce(jnp.maximum, tops)
    shares = [jnp.exp(t - top_all) for t in tops]
    mass_all = sum(shares[n] * stat_ref[n, 1:2] for n in range(PAIR))
    inner_all = sum(shares[n] * stat_ref[n, 2:3] for n in range(PAIR))
    over = 1.0 / mass_all
    weights = weights * (jnp.exp(top - top_all) * over)
    rounded = weights.astype(jnp.bfloat16)
    grad_scores = (weights * (grad_weights - inner_all * over)).astype(jnp.bfloat16)
    part_ref[:, :, 0] = (dot(grad_scores, queries, plain) * INV).astype(jnp.bfloat16).reshape(SLOTS, 2, QUARTER, D)
    part_ref[:, :, 1] = dot(rounded, grads, plain).astype(jnp.bfloat16).reshape(SLOTS, 2, QUARTER, D)

    def send_back(slot, to, at, may_be_self=False):
        far_plane = pltpu.make_async_remote_copy(
            src_ref=part_ref.at[slot, 1 - p], dst_ref=back_ref.at[p, to], send_sem=back_send, recv_sem=back_sem,
            device_id=(at, across), device_id_type=MESH,
        )
        far_plane.start()
        sent.append(far_plane)
        remote = pltpu.make_async_remote_copy(
            src_ref=part_ref.at[slot, p], dst_ref=back_ref.at[p, to], send_sem=back_send, recv_sem=back_sem,
            device_id=(at, h), device_id_type=MESH,
        )
        if may_be_self:
            local = pltpu.make_async_copy(part_ref.at[slot, p], back_ref.at[p, to], back_sem)
            pl.when(at != d)(remote.start)
            pl.when(at == d)(local.start)
            sent_maybe.append((at, remote))
        else:
            remote.start()
            sent.append(remote)

    for k, at in zip(ODD_STEPS[::-1], odd_with[::-1]):
        send_back(8 - 2 * k, k - 1, at, may_be_self=True)
    for k, at in zip(EVEN_STEPS[::-1], even_from[::-1]):
        send_back(7 - 2 * k, 4 + k, at)
    for n, at in enumerate(far):
        send_back(RECALL + n, 8 + c, at)
    send_back(OTHER, 4, other_core)
    own_across = pltpu.make_async_remote_copy(
        src_ref=part_ref.at[OWN, 1 - p], dst_ref=back_ref.at[p, 10], send_sem=back_send, recv_sem=back_sem,
        device_id=(d, across), device_id_type=MESH,
    )
    own_across.start()
    sent.append(own_across)
    pltpu.make_async_copy(part_ref.at[OWN, p], back_ref.at[p, 10], back_sem).start()

    out = dot(rounded, values, first)
    grad_queries = dot(grad_scores, keys, first) * INV
    rows_ref[:, :, 0] = out.astype(jnp.bfloat16).reshape(PAIR, 2, C, D)
    rows_ref[:, :, 1] = grad_queries.astype(jnp.bfloat16).reshape(PAIR, 2, C, D)
    pltpu.make_async_copy(rows_ref.at[b, 0], got_ref.at[b, 0], rows_sem).start()
    for of, which, to in ((1 - b, 0, (d, mate)), (1 - b, 1, (other_core, mate)), (b, 1, (other_core, h))):
        remote = pltpu.make_async_remote_copy(
            src_ref=rows_ref.at[of, which], dst_ref=got_ref.at[b, which], send_sem=rows_send, recv_sem=rows_sem,
            device_id=to, device_id_type=MESH,
        )
        remote.start()
        sent.append(remote)

    pltpu.make_async_copy(back_ref, back_ref, back_sem).wait()

    def read(n):
        return back_ref[0, n].astype(jnp.float32) + back_ref[1, n].astype(jnp.float32)

    recalled = read(8) + read(9)
    to_even = jnp.where(late == c, 1.0, 0.0)
    even_total = read(10) + read(5) + read(6) + read(7) + recalled * to_even
    odd_total = read(4) + read(0) + read(1) + read(2) + read(3) + recalled * (1.0 - to_even)
    sums_out[h, c] = even_total.astype(jnp.bfloat16)
    sums_out[h, 1 - c] = odd_total.astype(jnp.bfloat16)
    sum_sends = [
        pltpu.make_async_remote_copy(
            src_ref=sums_out.at[h], dst_ref=sums_out.at[h], send_sem=sums_send.at[k], recv_sem=sums_sem.at[k],
            device_id=(d, at), device_id_type=MESH,
        )
        for k, at in enumerate(heads)
    ]
    for copy in sum_sends:
        copy.start()

    pltpu.make_async_copy(got_ref, got_ref, rows_sem).wait()
    for which, place in ((0, c), (1, 1 - c)):
        total = sum(got_ref[n, which].astype(jnp.float32) for n in range(PAIR))
        for n in range(2):
            rows_out[n, place] = total[n].astype(jnp.bfloat16)

    for copy in sent:
        copy.wait_send()
    for at, copy in sent_maybe:
        pl.when(at != d)(copy.wait_send)
    for copy in sum_sends:
        copy.wait_send()
        copy.wait_recv()


def lay_out_kernel(rows_ref, sums_ref, out_ref, dq_ref, dk_ref, dv_ref):
    out_ref[...] = rows_ref[0].reshape(2 * C, D)
    dq_ref[...] = rows_ref[1].reshape(2 * C, D)
    for h in range(HEADS):
        g, q = h // GROUP, 2 * (h % PAIR) + h // PAIR % 2
        for s in range(2):
            rows = slice(s * C + q * QUARTER, s * C + (q + 1) * QUARTER)
            dk_ref[g, rows] = sums_ref[h, s, 0]
            dv_ref[g, rows] = sums_ref[h, s, 1]


def on_device(queries, keys, values, grad_out, episode_lengths, key_stretches):
    vmem = pl.BlockSpec(memory_space=pltpu.VMEM)
    dma = pltpu.SemaphoreType.DMA
    bf16 = jnp.bfloat16
    inputs = [
        pltpu.with_memory_space_constraint(x, pltpu.HBM)
        for x in (queries, keys, values, grad_out, episode_lengths, key_stretches.T)
    ]
    rows, sums = pl.pallas_call(
        attend_kernel,
        out_shape=(
            pltpu.VMEM((2, 2, C, D), bf16),
            pltpu.VMEM((HEADS, 2, 2, QUARTER, D), bf16),
        ),
        in_specs=[pl.BlockSpec(memory_space=pltpu.HBM)] * 6,
        out_specs=(vmem, vmem),
        scratch_shapes=[
            pltpu.VMEM((2, PAIR, 2, C, D), bf16),
            pltpu.VMEM((SLOTS, 2, HALF, D), bf16),
            pltpu.VMEM((SLOTS * HALF, 2 * C), jnp.float32),
            pltpu.VMEM((PAIR, 8, ROWS), jnp.float32),
            pltpu.VMEM((SLOTS, 2, 2, QUARTER, D), bf16),
            pltpu.VMEM((2, SLOTS, 2, QUARTER, D), bf16),
            pltpu.VMEM((PAIR, 2, 2, C, D), bf16),
            pltpu.VMEM((PAIR, 2, 2, C, D), bf16),
            pltpu.SMEM((HEADS,), jnp.int32),
            pltpu.SMEM((4, 2 * PAIRS), jnp.int32),
            dma((2,)), dma, dma, dma, dma, dma, dma((HEADS - 1,)),
            dma, dma, dma, dma, dma, dma((HEADS - 1,)),
        ],
        compiler_params=pltpu.CompilerParams(
            collective_id=0, has_side_effects=True, vmem_limit_bytes=16 * 1024 * 1024
        ),
        name="attend",
    )(*inputs)
    half = jax.ShapeDtypeStruct((2 * C, D), bf16)
    both = jax.ShapeDtypeStruct((2, 2 * C, D), bf16)
    return pl.pallas_call(
        lay_out_kernel,
        out_shape=(half, half, both, both),
        in_specs=[vmem] * 2,
        out_specs=(vmem,) * 4,
        name="lay_out",
    )(*(pltpu.with_memory_space_constraint(x, pltpu.VMEM) for x in (rows, sums)))


def solution(mesh):
    return jax.shard_map(
        on_device,
        mesh=mesh,
        in_specs=(
            P("ctx", "head"),
            P(None, "ctx", None),
            P(None, "ctx", None),
            P("ctx", "head"),
            P(),
            P(),
        ),
        out_specs=(P("ctx", "head"), P("ctx", "head"), P(None, "ctx", None), P(None, "ctx", None)),
        check_vma=False,
    )
```

```python
import functools
import math

import jax
import jax.numpy as jnp
from jax import lax
from jax.experimental import pallas as pl
from jax.experimental.pallas import tpu as pltpu
from jax.sharding import PartitionSpec as P

MESH = pl.DeviceIdType.MESH
C = 64
HALF = 32
QUARTER = 16
HEADS = 8
GROUP = 4
PAIR = 2
PAIRS = 64
ROWS = PAIR * 2 * C
CHIPS = 32
Z_CHIPS = 8
SLOTS = 11
OWN, OTHER, RECALL = 7, 8, 9
D = 128
MASKED = -1e30
EVEN_STEPS = (1, 2, 3)
ODD_STEPS = (1, 2, 3, 4)
INV = 1.0 / math.sqrt(D)


def device_of(pair):
    pair = lax.rem(pair + 2 * PAIRS, PAIRS)
    return jnp.where(pair < PAIRS // 2, 2 * pair, 2 * PAIRS - 1 - 2 * pair)


def attend_kernel(
    q_hbm, k_hbm, v_hbm, do_hbm, ep_hbm, ks_hbm,
    rows_out, sums_out,
    qdo_ref, kv_ref, bias_ref, stat_ref, part_ref, even_ref, odd_ref, recall_ref, acc_ref, rows_ref, got_ref,
    ep_ref, ks_ref,
    in_sems, kv_sem, q_sem, stat_sem, even_sem, odd_sem, recall_sem, rows_sem, sums_sem,
    kv_send, q_send, stat_send, back_send, rows_send, sums_send,
):
    d = lax.axis_index("ctx")
    h = lax.axis_index("head")
    m, c = d // 2, d % 2
    g, p, b = h // GROUP, h % PAIR, h // PAIR % 2
    mate = h + 2 - 4 * b
    across = h + 1 - 2 * p
    opposite = h + 4 - 8 * g
    mine = jnp.where(c == 0, m, PAIRS - 1 - m)
    other = PAIRS - 1 - mine
    other_core = 2 * m + 1 - c
    far_chip = lax.rem(m + CHIPS // 2, CHIPS)
    late = jnp.where(m >= CHIPS // 2, 1, 0)

    even_to = [device_of(mine + k) for k in EVEN_STEPS]
    even_from = [device_of(mine - k) for k in EVEN_STEPS]
    odd_with = [device_of(other + k) for k in ODD_STEPS]
    far = [2 * far_chip, 2 * far_chip + 1]
    heads = [(h + k) % HEADS for k in (4, 3, 5, 2, 6, 1, 7)]

    barrier = pltpu.get_barrier_semaphore()

    def greet(ctx_at, head_at):
        pl.semaphore_signal(barrier, inc=1, device_id=(ctx_at, head_at), device_id_type=MESH)

    for at in odd_with[::-1]:
        pl.when(at != d)(functools.partial(greet, at, h))
    for at in even_from[::-1] + far + [other_core]:
        greet(at, h)
    for at in (mate, across, opposite):
        greet(d, at)
    greet(other_core, mate)

    even_rows, odd_rows = pl.ds(c * C, C), pl.ds((1 - c) * C, C)
    loads = [
        pltpu.make_async_copy(ep_hbm, ep_ref, in_sems.at[0]),
        pltpu.make_async_copy(ks_hbm, ks_ref, in_sems.at[1]),
    ]
    own = [
        pltpu.make_async_copy(q_hbm.at[even_rows], qdo_ref.at[0, b, 0], q_sem),
        pltpu.make_async_copy(do_hbm.at[even_rows], qdo_ref.at[1, b, 0], q_sem),
        pltpu.make_async_copy(k_hbm.at[g, pl.ds(c * C + b * HALF, HALF)], kv_ref.at[OWN, 0], kv_sem),
        pltpu.make_async_copy(v_hbm.at[g, pl.ds(c * C + b * HALF, HALF)], kv_ref.at[OWN, 1], kv_sem),
    ]
    for copy in loads + own:
        copy.start()

    self_count = jnp.where(lax.rem(mine, PAIRS // 2) < 2, 1, 0)
    pl.semaphore_wait(barrier, 4 + 3 + 2 + 1 + 3 + 1 - self_count)

    sent, sent_maybe = [], []

    def send_kv(stretch, slot, at, may_be_self=False):
        rows = pl.ds(stretch * C + b * HALF, HALF)
        for which, ref in enumerate((k_hbm, v_hbm)):
            remote = pltpu.make_async_remote_copy(
                src_ref=ref.at[g, rows], dst_ref=kv_ref.at[slot, which], send_sem=kv_send, recv_sem=kv_sem,
                device_id=(at, h), device_id_type=MESH,
            )
            if may_be_self:
                local = pltpu.make_async_copy(ref.at[g, rows], kv_ref.at[slot, which], kv_sem)
                pl.when(at != d)(remote.start)
                pl.when(at == d)(local.start)
                sent_maybe.append((at, remote))
            else:
                remote.start()
                sent.append(remote)

    def send_q(rows, which, to):
        for n, ref in enumerate((q_hbm, do_hbm)):
            remote = pltpu.make_async_remote_copy(
                src_ref=ref.at[rows], dst_ref=qdo_ref.at[n, b, which], send_sem=q_send, recv_sem=q_sem,
                device_id=to, device_id_type=MESH,
            )
            remote.start()
            sent.append(remote)

    for k, at in zip(ODD_STEPS[::-1], odd_with[::-1]):
        send_kv(1 - c, 8 - 2 * k, at, may_be_self=True)
    for k, at in zip(EVEN_STEPS[::-1], even_to[::-1]):
        send_kv(c, 7 - 2 * k, at)
    for at in far:
        send_kv(late, RECALL + c, at)
    send_kv(1 - c, OTHER, other_core)
    send_q(even_rows, 0, (d, mate))
    send_q(odd_rows, 1, (other_core, mate))
    send_q(odd_rows, 1, (other_core, h))

    for copy in loads:
        copy.wait()
    lane = lax.broadcasted_iota(jnp.int32, (1, 2 * C), 1)
    query_pos = 2 * mine * C + lane
    first_pos = jnp.zeros_like(query_pos)
    start = jnp.int32(0)
    for e in range(HEADS - 1):
        start = start + ep_ref[e]
        first_pos = jnp.where(start <= query_pos, start, first_pos)
    row_of = (2 * d + c, 2 * other_core + c)
    entries = [[ks_ref[e, row] for e in range(4)] for row in row_of]
    far_valid = jnp.logical_or(late == 1, c == 1)
    key_row = lax.broadcasted_iota(jnp.int32, (HALF, 2 * C), 0) + b * HALF
    for slot in range(SLOTS):
        if slot < RECALL:
            stretch = 2 * mine - 7 + slot
        else:
            at = far[slot - RECALL]
            stretch = jnp.where(far_valid, jnp.where(late == 1, at, 2 * PAIRS - 1 - at), -1)
        base = []
        for row in entries:
            hit = row[0] == stretch
            for entry in row[1:]:
                hit = jnp.logical_or(hit, entry == stretch)
            base.append(jnp.where(hit, stretch * C, -(1 << 20)))
        key_pos = key_row + jnp.where(lane < C, base[0], base[1])
        seen = (key_pos >= first_pos) & (key_pos <= query_pos)
        bias_ref[pl.ds(slot * HALF, HALF), :] = jnp.where(seen, 0.0, MASKED)

    pltpu.make_async_copy(qdo_ref, qdo_ref, q_sem).wait()
    pltpu.make_async_copy(kv_ref, kv_ref, kv_sem).wait()

    queries = qdo_ref[0].reshape(ROWS, D)
    grads = qdo_ref[1].reshape(ROWS, D)
    keys = kv_ref[:, 0].reshape(SLOTS * HALF, D)
    values = kv_ref[:, 1].reshape(SLOTS * HALF, D)
    last = (((1,), (1,)), ((), ()))
    first = (((0,), (0,)), ((), ()))
    plain = (((1,), (0,)), ((), ()))

    def dot(a, b, dims):
        return lax.dot_general(a, b, dims, preferred_element_type=jnp.float32)

    scores = dot(keys, queries, last) * INV + jnp.concatenate([bias_ref[...]] * PAIR, axis=1)
    top = jnp.max(scores, axis=0, keepdims=True)
    weights = jnp.exp(scores - top)
    mass = jnp.sum(weights, axis=0, keepdims=True)
    grad_weights = dot(values, grads, last)
    inner = jnp.sum(weights * grad_weights, axis=0, keepdims=True)

    stat_ref[b, 0:1] = top
    stat_ref[b, 1:2] = mass
    stat_ref[b, 2:3] = inner
    remote = pltpu.make_async_remote_copy(
        src_ref=stat_ref.at[b], dst_ref=stat_ref.at[b], send_sem=stat_send, recv_sem=stat_sem,
        device_id=(d, mate), device_id_type=MESH,
    )
    remote.start()
    sent.append(remote)
    remote.wait_recv()
    tops = [stat_ref[n, 0:1] for n in range(PAIR)]
    top_all = functools.reduce(jnp.maximum, tops)
    shares = [jnp.exp(t - top_all) for t in tops]
    mass_all = sum(shares[n] * stat_ref[n, 1:2] for n in range(PAIR))
    inner_all = sum(shares[n] * stat_ref[n, 2:3] for n in range(PAIR))
    over = 1.0 / mass_all
    weights = weights * (jnp.exp(top - top_all) * over)
    rounded = weights.astype(jnp.bfloat16)
    grad_scores = (weights * (grad_weights - inner_all * over)).astype(jnp.bfloat16)
    part_ref[:, :, 0] = (dot(grad_scores, queries, plain) * INV).astype(jnp.bfloat16).reshape(SLOTS, 2, QUARTER, D)
    part_ref[:, :, 1] = dot(rounded, grads, plain).astype(jnp.bfloat16).reshape(SLOTS, 2, QUARTER, D)

    def send_back(slot, buffer, sem, to, at, may_be_self=False):
        far_plane = pltpu.make_async_remote_copy(
            src_ref=part_ref.at[slot, 1 - p], dst_ref=buffer.at[p, to], send_sem=back_send, recv_sem=sem,
            device_id=(at, across), device_id_type=MESH,
        )
        far_plane.start()
        sent.append(far_plane)
        remote = pltpu.make_async_remote_copy(
            src_ref=part_ref.at[slot, p], dst_ref=buffer.at[p, to], send_sem=back_send, recv_sem=sem,
            device_id=(at, h), device_id_type=MESH,
        )
        if may_be_self:
            local = pltpu.make_async_copy(part_ref.at[slot, p], buffer.at[p, to], sem)
            pl.when(at != d)(remote.start)
            pl.when(at == d)(local.start)
            sent_maybe.append((at, remote))
        else:
            remote.start()
            sent.append(remote)

    for k, at in zip(ODD_STEPS[::-1], odd_with[::-1]):
        send_back(8 - 2 * k, odd_ref, odd_sem, k - 1, at, may_be_self=True)
    for k, at in zip(EVEN_STEPS[::-1], even_from[::-1]):
        send_back(7 - 2 * k, even_ref, even_sem, k - 1, at)
    for n, at in enumerate(far):
        send_back(RECALL + n, recall_ref, recall_sem, c, at)
    send_back(OTHER, odd_ref, odd_sem, 4, other_core)
    own_across = pltpu.make_async_remote_copy(
        src_ref=part_ref.at[OWN, 1 - p], dst_ref=even_ref.at[p, 3], send_sem=back_send, recv_sem=even_sem,
        device_id=(d, across), device_id_type=MESH,
    )
    own_across.start()
    sent.append(own_across)
    pltpu.make_async_copy(part_ref.at[OWN, p], even_ref.at[p, 3], even_sem).start()

    out = dot(rounded, values, first)
    grad_queries = dot(grad_scores, keys, first) * INV
    rows_ref[:, :, 0] = out.astype(jnp.bfloat16).reshape(PAIR, 2, C, D)
    rows_ref[:, :, 1] = grad_queries.astype(jnp.bfloat16).reshape(PAIR, 2, C, D)
    pltpu.make_async_copy(rows_ref.at[b, 0], got_ref.at[b, 0], rows_sem).start()
    for of, which, to in ((1 - b, 0, (d, mate)), (1 - b, 1, (other_core, mate)), (b, 1, (other_core, h))):
        remote = pltpu.make_async_remote_copy(
            src_ref=rows_ref.at[of, which], dst_ref=got_ref.at[b, which], send_sem=rows_send, recv_sem=rows_sem,
            device_id=to, device_id_type=MESH,
        )
        remote.start()
        sent.append(remote)

    sum_sends = []

    def add_up(buffer, sem, start):
        pltpu.make_async_copy(buffer, buffer, sem).wait()
        total = jnp.sum(buffer[...].astype(jnp.float32), axis=(0, 1))
        acc_ref[...] = total if start else acc_ref[...] + total

    first_place = lax.rem(m, Z_CHIPS) // (Z_CHIPS // 2)
    for turn, place in enumerate((first_place, 1 - first_place)):
        pl.when(place == c)(functools.partial(add_up, even_ref, even_sem, True))
        pl.when(place != c)(functools.partial(add_up, odd_ref, odd_sem, True))
        pl.when(place == late)(functools.partial(add_up, recall_ref, recall_sem, False))
        sums_out[h, place] = acc_ref[...].astype(jnp.bfloat16)
        for k, at in enumerate(heads):
            remote = pltpu.make_async_remote_copy(
                src_ref=sums_out.at[h, place], dst_ref=sums_out.at[h, place],
                send_sem=sums_send.at[turn, k], recv_sem=sums_sem.at[turn, k],
                device_id=(d, at), device_id_type=MESH,
            )
            remote.start()
            sum_sends.append(remote)

    pltpu.make_async_copy(got_ref, got_ref, rows_sem).wait()
    for which, place in ((0, c), (1, 1 - c)):
        total = sum(got_ref[n, which].astype(jnp.float32) for n in range(PAIR))
        for n in range(2):
            rows_out[n, place] = total[n].astype(jnp.bfloat16)

    for copy in sent:
        copy.wait_send()
    for at, copy in sent_maybe:
        pl.when(at != d)(copy.wait_send)
    for copy in sum_sends:
        copy.wait_send()
        copy.wait_recv()


def lay_out_kernel(rows_ref, sums_ref, out_ref, dq_ref, dk_ref, dv_ref):
    out_ref[...] = rows_ref[0].reshape(2 * C, D)
    dq_ref[...] = rows_ref[1].reshape(2 * C, D)
    for h in range(HEADS):
        g, q = divmod(h, GROUP)
        for s in range(2):
            rows = slice(s * C + q * QUARTER, s * C + (q + 1) * QUARTER)
            dk_ref[g, rows] = sums_ref[h, s, 0]
            dv_ref[g, rows] = sums_ref[h, s, 1]


def on_device(queries, keys, values, grad_out, episode_lengths, key_stretches):
    vmem = pl.BlockSpec(memory_space=pltpu.VMEM)
    dma = pltpu.SemaphoreType.DMA
    bf16 = jnp.bfloat16
    inputs = [
        pltpu.with_memory_space_constraint(x, pltpu.HBM)
        for x in (queries, keys, values, grad_out, episode_lengths, key_stretches.T)
    ]
    rows, sums = pl.pallas_call(
        attend_kernel,
        out_shape=(
            pltpu.VMEM((2, 2, C, D), bf16),
            pltpu.VMEM((HEADS, 2, 2, QUARTER, D), bf16),
        ),
        in_specs=[pl.BlockSpec(memory_space=pltpu.HBM)] * 6,
        out_specs=(vmem, vmem),
        scratch_shapes=[
            pltpu.VMEM((2, PAIR, 2, C, D), bf16),
            pltpu.VMEM((SLOTS, 2, HALF, D), bf16),
            pltpu.VMEM((SLOTS * HALF, 2 * C), jnp.float32),
            pltpu.VMEM((PAIR, 8, ROWS), jnp.float32),
            pltpu.VMEM((SLOTS, 2, 2, QUARTER, D), bf16),
            pltpu.VMEM((2, 4, 2, QUARTER, D), bf16),
            pltpu.VMEM((2, 5, 2, QUARTER, D), bf16),
            pltpu.VMEM((2, 2, 2, QUARTER, D), bf16),
            pltpu.VMEM((2, QUARTER, D), jnp.float32),
            pltpu.VMEM((PAIR, 2, 2, C, D), bf16),
            pltpu.VMEM((PAIR, 2, 2, C, D), bf16),
            pltpu.SMEM((HEADS,), jnp.int32),
            pltpu.SMEM((4, 2 * PAIRS), jnp.int32),
            dma((2,)), dma, dma, dma, dma, dma, dma, dma, dma((2, HEADS - 1)),
            dma, dma, dma, dma, dma, dma((2, HEADS - 1)),
        ],
        compiler_params=pltpu.CompilerParams(
            collective_id=0, has_side_effects=True, vmem_limit_bytes=16 * 1024 * 1024
        ),
        name="attend",
    )(*inputs)
    half = jax.ShapeDtypeStruct((2 * C, D), bf16)
    both = jax.ShapeDtypeStruct((2, 2 * C, D), bf16)
    return pl.pallas_call(
        lay_out_kernel,
        out_shape=(half, half, both, both),
        in_specs=[vmem] * 2,
        out_specs=(vmem,) * 4,
        name="lay_out",
    )(*(pltpu.with_memory_space_constraint(x, pltpu.VMEM) for x in (rows, sums)))


def solution(mesh):
    return jax.shard_map(
        on_device,
        mesh=mesh,
        in_specs=(
            P("ctx", "head"),
            P(None, "ctx", None),
            P(None, "ctx", None),
            P("ctx", "head"),
            P(),
            P(),
        ),
        out_specs=(P("ctx", "head"), P("ctx", "head"), P(None, "ctx", None), P(None, "ctx", None)),
        check_vma=False,
    )
```

```python
import functools
import math

import jax
import jax.numpy as jnp
from jax import lax
from jax.experimental import pallas as pl
from jax.experimental.pallas import tpu as pltpu
from jax.sharding import PartitionSpec as P

MESH = pl.DeviceIdType.MESH
C = 64
HALF = 32
QUARTER = 16
HEADS = 8
GROUP = 4
PAIR = 2
PAIRS = 64
ROWS = PAIR * 2 * C
CHIPS = 32
Z_CHIPS = 8
SLOTS = 11
OWN, OTHER, RECALL = 7, 8, 9
D = 128
MASKED = -1e30
EVEN_STEPS = (1, 2, 3)
ODD_STEPS = (1, 2, 3, 4)
INV = 1.0 / math.sqrt(D)


def device_of(pair):
    pair = lax.rem(pair + 2 * PAIRS, PAIRS)
    return jnp.where(pair < PAIRS // 2, 2 * pair, 2 * PAIRS - 1 - 2 * pair)


def attend_kernel(
    q_hbm, k_hbm, v_hbm, do_hbm, ep_hbm, ks_hbm,
    rows_out, sums_out,
    qdo_ref, kv_ref, bias_ref, stat_ref, part_ref, even_ref, odd_ref, recall_ref, acc_ref, rows_ref, got_ref,
    ep_ref, ks_ref,
    in_sems, kv_sem, q_sem, stat_sem, even_sem, odd_sem, recall_sem, rows_sem, sums_sem,
    kv_send, q_send, stat_send, back_send, rows_send, sums_send, opposite_sem,
):
    d = lax.axis_index("ctx")
    h = lax.axis_index("head")
    m, c = d // 2, d % 2
    g, p, b = h // GROUP, h % PAIR, h // PAIR % 2
    mate = h + 2 - 4 * b
    across = h + 1 - 2 * p
    opposite = h + 4 - 8 * g
    mine = jnp.where(c == 0, m, PAIRS - 1 - m)
    other = PAIRS - 1 - mine
    other_core = 2 * m + 1 - c
    far_chip = lax.rem(m + CHIPS // 2, CHIPS)
    late = jnp.where(m >= CHIPS // 2, 1, 0)

    even_to = [device_of(mine + k) for k in EVEN_STEPS]
    even_from = [device_of(mine - k) for k in EVEN_STEPS]
    odd_with = [device_of(other + k) for k in ODD_STEPS]
    far = [2 * far_chip, 2 * far_chip + 1]
    heads = [(h + k) % HEADS for k in (4, 3, 5, 2, 6, 1, 7)]

    barrier = pltpu.get_barrier_semaphore()

    def greet(ctx_at, head_at):
        pl.semaphore_signal(barrier, inc=1, device_id=(ctx_at, head_at), device_id_type=MESH)

    for at in odd_with[::-1]:
        pl.when(at != d)(functools.partial(greet, at, h))
    for at in even_from[::-1] + far + [other_core]:
        greet(at, h)
    for at in (mate, across):
        greet(d, at)
    pl.when(g == 0)(functools.partial(greet, d, opposite))
    greet(other_core, mate)

    even_rows, odd_rows = pl.ds(c * C, C), pl.ds((1 - c) * C, C)
    loads = [
        pltpu.make_async_copy(ep_hbm, ep_ref, in_sems.at[0]),
        pltpu.make_async_copy(ks_hbm, ks_ref, in_sems.at[1]),
    ]
    own = [
        pltpu.make_async_copy(q_hbm.at[even_rows], qdo_ref.at[0, b, 0], q_sem),
        pltpu.make_async_copy(do_hbm.at[even_rows], qdo_ref.at[1, b, 0], q_sem),
        pltpu.make_async_copy(k_hbm.at[g, pl.ds(c * C + b * HALF, HALF)], kv_ref.at[OWN, 0], kv_sem),
        pltpu.make_async_copy(v_hbm.at[g, pl.ds(c * C + b * HALF, HALF)], kv_ref.at[OWN, 1], kv_sem),
    ]
    for copy in loads + own:
        copy.start()

    self_count = jnp.where(lax.rem(mine, PAIRS // 2) < 2, 1, 0)
    pl.semaphore_wait(barrier, 4 + 3 + 2 + 1 + 2 + 1 + g - self_count)

    sent, sent_maybe = [], []

    def send_kv(stretch, slot, at, may_be_self=False):
        rows = pl.ds(stretch * C + b * HALF, HALF)
        for which, ref in enumerate((k_hbm, v_hbm)):
            remote = pltpu.make_async_remote_copy(
                src_ref=ref.at[g, rows], dst_ref=kv_ref.at[slot, which], send_sem=kv_send, recv_sem=kv_sem,
                device_id=(at, h), device_id_type=MESH,
            )
            if may_be_self:
                local = pltpu.make_async_copy(ref.at[g, rows], kv_ref.at[slot, which], kv_sem)
                pl.when(at != d)(remote.start)
                pl.when(at == d)(local.start)
                sent_maybe.append((at, remote))
            else:
                remote.start()
                sent.append(remote)

    def send_q(rows, which, to):
        for n, ref in enumerate((q_hbm, do_hbm)):
            remote = pltpu.make_async_remote_copy(
                src_ref=ref.at[rows], dst_ref=qdo_ref.at[n, b, which], send_sem=q_send, recv_sem=q_sem,
                device_id=to, device_id_type=MESH,
            )
            remote.start()
            sent.append(remote)

    for k, at in zip(ODD_STEPS[::-1], odd_with[::-1]):
        send_kv(1 - c, 8 - 2 * k, at, may_be_self=True)
    for k, at in zip(EVEN_STEPS[::-1], even_to[::-1]):
        send_kv(c, 7 - 2 * k, at)
    for at in far:
        send_kv(late, RECALL + c, at)
    send_kv(1 - c, OTHER, other_core)
    send_q(even_rows, 0, (d, mate))
    send_q(odd_rows, 1, (other_core, mate))
    send_q(odd_rows, 1, (other_core, h))

    for copy in loads:
        copy.wait()
    lane = lax.broadcasted_iota(jnp.int32, (1, 2 * C), 1)
    query_pos = 2 * mine * C + lane
    first_pos = jnp.zeros_like(query_pos)
    start = jnp.int32(0)
    for e in range(HEADS - 1):
        start = start + ep_ref[e]
        first_pos = jnp.where(start <= query_pos, start, first_pos)
    row_of = (2 * d + c, 2 * other_core + c)
    entries = [[ks_ref[e, row] for e in range(4)] for row in row_of]
    far_valid = jnp.logical_or(late == 1, c == 1)
    key_row = lax.broadcasted_iota(jnp.int32, (HALF, 2 * C), 0) + b * HALF
    for slot in range(SLOTS):
        if slot < RECALL:
            stretch = 2 * mine - 7 + slot
        else:
            at = far[slot - RECALL]
            stretch = jnp.where(far_valid, jnp.where(late == 1, at, 2 * PAIRS - 1 - at), -1)
        base = []
        for row in entries:
            hit = row[0] == stretch
            for entry in row[1:]:
                hit = jnp.logical_or(hit, entry == stretch)
            base.append(jnp.where(hit, stretch * C, -(1 << 20)))
        key_pos = key_row + jnp.where(lane < C, base[0], base[1])
        seen = (key_pos >= first_pos) & (key_pos <= query_pos)
        bias_ref[pl.ds(slot * HALF, HALF), :] = jnp.where(seen, 0.0, MASKED)

    pltpu.make_async_copy(qdo_ref, qdo_ref, q_sem).wait()
    pltpu.make_async_copy(kv_ref, kv_ref, kv_sem).wait()

    queries = qdo_ref[0].reshape(ROWS, D)
    grads = qdo_ref[1].reshape(ROWS, D)
    keys = kv_ref[:, 0].reshape(SLOTS * HALF, D)
    values = kv_ref[:, 1].reshape(SLOTS * HALF, D)
    last = (((1,), (1,)), ((), ()))
    first = (((0,), (0,)), ((), ()))
    plain = (((1,), (0,)), ((), ()))

    def dot(a, b, dims):
        return lax.dot_general(a, b, dims, preferred_element_type=jnp.float32)

    scores = dot(keys, queries, last) * INV + jnp.concatenate([bias_ref[...]] * PAIR, axis=1)
    top = jnp.max(scores, axis=0, keepdims=True)
    weights = jnp.exp(scores - top)
    mass = jnp.sum(weights, axis=0, keepdims=True)
    grad_weights = dot(values, grads, last)
    inner = jnp.sum(weights * grad_weights, axis=0, keepdims=True)

    stat_ref[b, 0:1] = top
    stat_ref[b, 1:2] = mass
    stat_ref[b, 2:3] = inner
    remote = pltpu.make_async_remote_copy(
        src_ref=stat_ref.at[b], dst_ref=stat_ref.at[b], send_sem=stat_send, recv_sem=stat_sem,
        device_id=(d, mate), device_id_type=MESH,
    )
    remote.start()
    sent.append(remote)
    remote.wait_recv()
    @pl.when(g == 1)
    def _():
        pl.semaphore_signal(opposite_sem, inc=1, device_id=(d, opposite), device_id_type=MESH)

    tops = [stat_ref[n, 0:1] for n in range(PAIR)]
    top_all = functools.reduce(jnp.maximum, tops)
    shares = [jnp.exp(t - top_all) for t in tops]
    mass_all = sum(shares[n] * stat_ref[n, 1:2] for n in range(PAIR))
    inner_all = sum(shares[n] * stat_ref[n, 2:3] for n in range(PAIR))
    over = 1.0 / mass_all
    weights = weights * (jnp.exp(top - top_all) * over)
    rounded = weights.astype(jnp.bfloat16)
    grad_scores = (weights * (grad_weights - inner_all * over)).astype(jnp.bfloat16)
    part_ref[:, :, 0] = (dot(grad_scores, queries, plain) * INV).astype(jnp.bfloat16).reshape(SLOTS, 2, QUARTER, D)
    part_ref[:, :, 1] = dot(rounded, grads, plain).astype(jnp.bfloat16).reshape(SLOTS, 2, QUARTER, D)

    def send_back(slot, buffer, sem, to, at, may_be_self=False):
        far_plane = pltpu.make_async_remote_copy(
            src_ref=part_ref.at[slot, 1 - p], dst_ref=buffer.at[p, to], send_sem=back_send, recv_sem=sem,
            device_id=(at, across), device_id_type=MESH,
        )
        far_plane.start()
        sent.append(far_plane)
        remote = pltpu.make_async_remote_copy(
            src_ref=part_ref.at[slot, p], dst_ref=buffer.at[p, to], send_sem=back_send, recv_sem=sem,
            device_id=(at, h), device_id_type=MESH,
        )
        if may_be_self:
            local = pltpu.make_async_copy(part_ref.at[slot, p], buffer.at[p, to], sem)
            pl.when(at != d)(remote.start)
            pl.when(at == d)(local.start)
            sent_maybe.append((at, remote))
        else:
            remote.start()
            sent.append(remote)

    for k, at in zip(ODD_STEPS[::-1], odd_with[::-1]):
        send_back(8 - 2 * k, odd_ref, odd_sem, k - 1, at, may_be_self=True)
    for k, at in zip(EVEN_STEPS[::-1], even_from[::-1]):
        send_back(7 - 2 * k, even_ref, even_sem, k - 1, at)
    for n, at in enumerate(far):
        send_back(RECALL + n, recall_ref, recall_sem, c, at)
    send_back(OTHER, odd_ref, odd_sem, 4, other_core)
    own_across = pltpu.make_async_remote_copy(
        src_ref=part_ref.at[OWN, 1 - p], dst_ref=even_ref.at[p, 3], send_sem=back_send, recv_sem=even_sem,
        device_id=(d, across), device_id_type=MESH,
    )
    own_across.start()
    sent.append(own_across)
    pltpu.make_async_copy(part_ref.at[OWN, p], even_ref.at[p, 3], even_sem).start()

    out = dot(rounded, values, first)
    grad_queries = dot(grad_scores, keys, first) * INV
    rows_ref[:, :, 0] = out.astype(jnp.bfloat16).reshape(PAIR, 2, C, D)
    rows_ref[:, :, 1] = grad_queries.astype(jnp.bfloat16).reshape(PAIR, 2, C, D)
    pltpu.make_async_copy(rows_ref.at[b, 0], got_ref.at[b, 0], rows_sem).start()
    for of, which, to in ((1 - b, 0, (d, mate)), (1 - b, 1, (other_core, mate)), (b, 1, (other_core, h))):
        remote = pltpu.make_async_remote_copy(
            src_ref=rows_ref.at[of, which], dst_ref=got_ref.at[b, which], send_sem=rows_send, recv_sem=rows_sem,
            device_id=to, device_id_type=MESH,
        )
        remote.start()
        sent.append(remote)

    sum_sends = []

    def add_up(buffer, sem, start):
        pltpu.make_async_copy(buffer, buffer, sem).wait()
        total = jnp.sum(buffer[...].astype(jnp.float32), axis=(0, 1))
        acc_ref[...] = total if start else acc_ref[...] + total

    pl.when(g == 0)(lambda: pl.semaphore_wait(opposite_sem, 1))
    for turn, place in enumerate((1, 0)):
        pl.when(place == c)(functools.partial(add_up, even_ref, even_sem, True))
        pl.when(place != c)(functools.partial(add_up, odd_ref, odd_sem, True))
        pl.when(place == late)(functools.partial(add_up, recall_ref, recall_sem, False))
        sums_out[h, place] = acc_ref[...].astype(jnp.bfloat16)
        for k, at in enumerate(heads):
            remote = pltpu.make_async_remote_copy(
                src_ref=sums_out.at[h, place], dst_ref=sums_out.at[h, place],
                send_sem=sums_send.at[turn, k], recv_sem=sums_sem.at[turn, k],
                device_id=(d, at), device_id_type=MESH,
            )
            remote.start()
            sum_sends.append(remote)

    pltpu.make_async_copy(got_ref, got_ref, rows_sem).wait()
    for which, place in ((0, c), (1, 1 - c)):
        total = sum(got_ref[n, which].astype(jnp.float32) for n in range(PAIR))
        for n in range(2):
            rows_out[n, place] = total[n].astype(jnp.bfloat16)

    for copy in sent:
        copy.wait_send()
    for at, copy in sent_maybe:
        pl.when(at != d)(copy.wait_send)
    for copy in sum_sends:
        copy.wait_send()
        copy.wait_recv()


def lay_out_kernel(rows_ref, sums_ref, out_ref, dq_ref, dk_ref, dv_ref):
    out_ref[...] = rows_ref[0].reshape(2 * C, D)
    dq_ref[...] = rows_ref[1].reshape(2 * C, D)
    for h in range(HEADS):
        g, q = divmod(h, GROUP)
        for s in range(2):
            rows = slice(s * C + q * QUARTER, s * C + (q + 1) * QUARTER)
            dk_ref[g, rows] = sums_ref[h, s, 0]
            dv_ref[g, rows] = sums_ref[h, s, 1]


def on_device(queries, keys, values, grad_out, episode_lengths, key_stretches):
    vmem = pl.BlockSpec(memory_space=pltpu.VMEM)
    dma = pltpu.SemaphoreType.DMA
    bf16 = jnp.bfloat16
    inputs = [
        pltpu.with_memory_space_constraint(x, pltpu.HBM)
        for x in (queries, keys, values, grad_out, episode_lengths, key_stretches.T)
    ]
    rows, sums = pl.pallas_call(
        attend_kernel,
        out_shape=(
            pltpu.VMEM((2, 2, C, D), bf16),
            pltpu.VMEM((HEADS, 2, 2, QUARTER, D), bf16),
        ),
        in_specs=[pl.BlockSpec(memory_space=pltpu.HBM)] * 6,
        out_specs=(vmem, vmem),
        scratch_shapes=[
            pltpu.VMEM((2, PAIR, 2, C, D), bf16),
            pltpu.VMEM((SLOTS, 2, HALF, D), bf16),
            pltpu.VMEM((SLOTS * HALF, 2 * C), jnp.float32),
            pltpu.VMEM((PAIR, 8, ROWS), jnp.float32),
            pltpu.VMEM((SLOTS, 2, 2, QUARTER, D), bf16),
            pltpu.VMEM((2, 4, 2, QUARTER, D), bf16),
            pltpu.VMEM((2, 5, 2, QUARTER, D), bf16),
            pltpu.VMEM((2, 2, 2, QUARTER, D), bf16),
            pltpu.VMEM((2, QUARTER, D), jnp.float32),
            pltpu.VMEM((PAIR, 2, 2, C, D), bf16),
            pltpu.VMEM((PAIR, 2, 2, C, D), bf16),
            pltpu.SMEM((HEADS,), jnp.int32),
            pltpu.SMEM((4, 2 * PAIRS), jnp.int32),
            dma((2,)), dma, dma, dma, dma, dma, dma, dma, dma((2, HEADS - 1)),
            dma, dma, dma, dma, dma, dma((2, HEADS - 1)), pltpu.SemaphoreType.REGULAR,
        ],
        compiler_params=pltpu.CompilerParams(
            collective_id=0, has_side_effects=True, vmem_limit_bytes=16 * 1024 * 1024
        ),
        name="attend",
    )(*inputs)
    half = jax.ShapeDtypeStruct((2 * C, D), bf16)
    both = jax.ShapeDtypeStruct((2, 2 * C, D), bf16)
    return pl.pallas_call(
        lay_out_kernel,
        out_shape=(half, half, both, both),
        in_specs=[vmem] * 2,
        out_specs=(vmem,) * 4,
        name="lay_out",
    )(*(pltpu.with_memory_space_constraint(x, pltpu.VMEM) for x in (rows, sums)))


def solution(mesh):
    return jax.shard_map(
        on_device,
        mesh=mesh,
        in_specs=(
            P("ctx", "head"),
            P(None, "ctx", None),
            P(None, "ctx", None),
            P("ctx", "head"),
            P(),
            P(),
        ),
        out_specs=(P("ctx", "head"), P("ctx", "head"), P(None, "ctx", None), P(None, "ctx", None)),
        check_vma=False,
    )
```

```python
import functools
import math

import jax
import jax.numpy as jnp
from jax import lax
from jax.experimental import pallas as pl
from jax.experimental.pallas import tpu as pltpu
from jax.sharding import PartitionSpec as P

MESH = pl.DeviceIdType.MESH
C = 64
HALF = 32
QUARTER = 16
HEADS = 8
GROUP = 4
PAIR = 2
PAIRS = 64
ROWS = PAIR * 2 * C
CHIPS = 32
Z_CHIPS = 8
SLOTS = 11
OWN, OTHER, RECALL = 7, 8, 9
D = 128
MASKED = -1e30
EVEN_STEPS = (1, 2, 3)
ODD_STEPS = (1, 2, 3, 4)
INV = 1.0 / math.sqrt(D)


def device_of(pair):
    pair = lax.rem(pair + 2 * PAIRS, PAIRS)
    return jnp.where(pair < PAIRS // 2, 2 * pair, 2 * PAIRS - 1 - 2 * pair)


def attend_kernel(
    q_hbm, k_hbm, v_hbm, do_hbm, ep_hbm, ks_hbm,
    rows_out, sums_out,
    qdo_ref, kv_ref, bias_ref, stat_ref, part_ref, even_ref, odd_ref, recall_ref, acc_ref, rows_ref, got_ref,
    ep_ref, ks_ref,
    in_sems, kv_sem, q_sem, stat_sem, even_sem, odd_sem, recall_sem, rows_sem, sums_sem,
    kv_send, q_send, stat_send, back_send, rows_send, sums_send, opposite_sem,
):
    d = lax.axis_index("ctx")
    h = lax.axis_index("head")
    m, c = d // 2, d % 2
    g, p, b = h // GROUP, h % PAIR, h // PAIR % 2
    mate = h + 2 - 4 * b
    across = h + 1 - 2 * p
    opposite = h + 4 - 8 * g
    mine = jnp.where(c == 0, m, PAIRS - 1 - m)
    other = PAIRS - 1 - mine
    other_core = 2 * m + 1 - c
    far_chip = lax.rem(m + CHIPS // 2, CHIPS)
    late = jnp.where(m >= CHIPS // 2, 1, 0)

    even_to = [device_of(mine + k) for k in EVEN_STEPS]
    even_from = [device_of(mine - k) for k in EVEN_STEPS]
    odd_with = [device_of(other + k) for k in ODD_STEPS]
    far = [2 * far_chip, 2 * far_chip + 1]
    heads = [(1 - g) * GROUP + (h + k) % GROUP for k in (0, 1, 3, 2)] + [g * GROUP + (h + k) % GROUP for k in (2, 1, 3)]

    barrier = pltpu.get_barrier_semaphore()

    def greet(ctx_at, head_at):
        pl.semaphore_signal(barrier, inc=1, device_id=(ctx_at, head_at), device_id_type=MESH)

    for at in odd_with[::-1]:
        pl.when(at != d)(functools.partial(greet, at, h))
    for at in even_from[::-1] + far + [other_core]:
        greet(at, h)
    for at in (mate, across):
        greet(d, at)
    pl.when(g == 0)(functools.partial(greet, d, opposite))
    greet(other_core, mate)

    even_rows, odd_rows = pl.ds(c * C, C), pl.ds((1 - c) * C, C)
    loads = [
        pltpu.make_async_copy(ep_hbm, ep_ref, in_sems.at[0]),
        pltpu.make_async_copy(ks_hbm, ks_ref, in_sems.at[1]),
    ]
    own = [
        pltpu.make_async_copy(q_hbm.at[even_rows], qdo_ref.at[0, b, 0], q_sem),
        pltpu.make_async_copy(do_hbm.at[even_rows], qdo_ref.at[1, b, 0], q_sem),
        pltpu.make_async_copy(k_hbm.at[g, pl.ds(c * C + b * HALF, HALF)], kv_ref.at[OWN, 0], kv_sem),
        pltpu.make_async_copy(v_hbm.at[g, pl.ds(c * C + b * HALF, HALF)], kv_ref.at[OWN, 1], kv_sem),
    ]
    for copy in loads + own:
        copy.start()

    self_count = jnp.where(lax.rem(mine, PAIRS // 2) < 2, 1, 0)
    pl.semaphore_wait(barrier, 4 + 3 + 2 + 1 + 2 + 1 + g - self_count)

    sent, sent_maybe = [], []

    def send_kv(stretch, slot, at, may_be_self=False):
        rows = pl.ds(stretch * C + b * HALF, HALF)
        for which, ref in enumerate((k_hbm, v_hbm)):
            remote = pltpu.make_async_remote_copy(
                src_ref=ref.at[g, rows], dst_ref=kv_ref.at[slot, which], send_sem=kv_send, recv_sem=kv_sem,
                device_id=(at, h), device_id_type=MESH,
            )
            if may_be_self:
                local = pltpu.make_async_copy(ref.at[g, rows], kv_ref.at[slot, which], kv_sem)
                pl.when(at != d)(remote.start)
                pl.when(at == d)(local.start)
                sent_maybe.append((at, remote))
            else:
                remote.start()
                sent.append(remote)

    def send_q(rows, which, to):
        for n, ref in enumerate((q_hbm, do_hbm)):
            remote = pltpu.make_async_remote_copy(
                src_ref=ref.at[rows], dst_ref=qdo_ref.at[n, b, which], send_sem=q_send, recv_sem=q_sem,
                device_id=to, device_id_type=MESH,
            )
            remote.start()
            sent.append(remote)

    for k, at in zip(ODD_STEPS[::-1], odd_with[::-1]):
        send_kv(1 - c, 8 - 2 * k, at, may_be_self=True)
    for k, at in zip(EVEN_STEPS[::-1], even_to[::-1]):
        send_kv(c, 7 - 2 * k, at)
    for at in far:
        send_kv(late, RECALL + c, at)
    send_kv(1 - c, OTHER, other_core)
    send_q(even_rows, 0, (d, mate))
    send_q(odd_rows, 1, (other_core, mate))
    send_q(odd_rows, 1, (other_core, h))

    for copy in loads:
        copy.wait()
    lane = lax.broadcasted_iota(jnp.int32, (1, 2 * C), 1)
    query_pos = 2 * mine * C + lane
    first_pos = jnp.zeros_like(query_pos)
    start = jnp.int32(0)
    for e in range(HEADS - 1):
        start = start + ep_ref[e]
        first_pos = jnp.where(start <= query_pos, start, first_pos)
    row_of = (2 * d + c, 2 * other_core + c)
    entries = [[ks_ref[e, row] for e in range(4)] for row in row_of]
    far_valid = jnp.logical_or(late == 1, c == 1)
    key_row = lax.broadcasted_iota(jnp.int32, (HALF, 2 * C), 0) + b * HALF
    for slot in range(SLOTS):
        if slot < RECALL:
            stretch = 2 * mine - 7 + slot
        else:
            at = far[slot - RECALL]
            stretch = jnp.where(far_valid, jnp.where(late == 1, at, 2 * PAIRS - 1 - at), -1)
        base = []
        for row in entries:
            hit = row[0] == stretch
            for entry in row[1:]:
                hit = jnp.logical_or(hit, entry == stretch)
            base.append(jnp.where(hit, stretch * C, -(1 << 20)))
        key_pos = key_row + jnp.where(lane < C, base[0], base[1])
        seen = (key_pos >= first_pos) & (key_pos <= query_pos)
        bias_ref[pl.ds(slot * HALF, HALF), :] = jnp.where(seen, 0.0, MASKED)

    pltpu.make_async_copy(qdo_ref, qdo_ref, q_sem).wait()
    pltpu.make_async_copy(kv_ref, kv_ref, kv_sem).wait()

    queries = qdo_ref[0].reshape(ROWS, D)
    grads = qdo_ref[1].reshape(ROWS, D)
    keys = kv_ref[:, 0].reshape(SLOTS * HALF, D)
    values = kv_ref[:, 1].reshape(SLOTS * HALF, D)
    last = (((1,), (1,)), ((), ()))
    first = (((0,), (0,)), ((), ()))
    plain = (((1,), (0,)), ((), ()))

    def dot(a, b, dims):
        return lax.dot_general(a, b, dims, preferred_element_type=jnp.float32)

    scores = dot(keys, queries, last) * INV + jnp.concatenate([bias_ref[...]] * PAIR, axis=1)
    top = jnp.max(scores, axis=0, keepdims=True)
    weights = jnp.exp(scores - top)
    mass = jnp.sum(weights, axis=0, keepdims=True)
    grad_weights = dot(values, grads, last)
    inner = jnp.sum(weights * grad_weights, axis=0, keepdims=True)

    stat_ref[b, 0:1] = top
    stat_ref[b, 1:2] = mass
    stat_ref[b, 2:3] = inner
    remote = pltpu.make_async_remote_copy(
        src_ref=stat_ref.at[b], dst_ref=stat_ref.at[b], send_sem=stat_send, recv_sem=stat_sem,
        device_id=(d, mate), device_id_type=MESH,
    )
    remote.start()
    sent.append(remote)
    remote.wait_recv()
    @pl.when(g == 1)
    def _():
        pl.semaphore_signal(opposite_sem, inc=1, device_id=(d, opposite), device_id_type=MESH)

    tops = [stat_ref[n, 0:1] for n in range(PAIR)]
    top_all = functools.reduce(jnp.maximum, tops)
    shares = [jnp.exp(t - top_all) for t in tops]
    mass_all = sum(shares[n] * stat_ref[n, 1:2] for n in range(PAIR))
    inner_all = sum(shares[n] * stat_ref[n, 2:3] for n in range(PAIR))
    over = 1.0 / mass_all
    weights = weights * (jnp.exp(top - top_all) * over)
    rounded = weights.astype(jnp.bfloat16)
    grad_scores = (weights * (grad_weights - inner_all * over)).astype(jnp.bfloat16)
    part_ref[:, :, 0] = (dot(grad_scores, queries, plain) * INV).astype(jnp.bfloat16).reshape(SLOTS, 2, QUARTER, D)
    part_ref[:, :, 1] = dot(rounded, grads, plain).astype(jnp.bfloat16).reshape(SLOTS, 2, QUARTER, D)

    def send_back(slot, buffer, sem, to, at, may_be_self=False):
        far_plane = pltpu.make_async_remote_copy(
            src_ref=part_ref.at[slot, 1 - p], dst_ref=buffer.at[p, to], send_sem=back_send, recv_sem=sem,
            device_id=(at, across), device_id_type=MESH,
        )
        far_plane.start()
        sent.append(far_plane)
        remote = pltpu.make_async_remote_copy(
            src_ref=part_ref.at[slot, p], dst_ref=buffer.at[p, to], send_sem=back_send, recv_sem=sem,
            device_id=(at, h), device_id_type=MESH,
        )
        if may_be_self:
            local = pltpu.make_async_copy(part_ref.at[slot, p], buffer.at[p, to], sem)
            pl.when(at != d)(remote.start)
            pl.when(at == d)(local.start)
            sent_maybe.append((at, remote))
        else:
            remote.start()
            sent.append(remote)

    for k, at in zip(ODD_STEPS[::-1], odd_with[::-1]):
        send_back(8 - 2 * k, odd_ref, odd_sem, k - 1, at, may_be_self=True)
    for k, at in zip(EVEN_STEPS[::-1], even_from[::-1]):
        send_back(7 - 2 * k, even_ref, even_sem, k - 1, at)
    for n, at in enumerate(far):
        send_back(RECALL + n, recall_ref, recall_sem, c, at)
    send_back(OTHER, odd_ref, odd_sem, 4, other_core)
    own_across = pltpu.make_async_remote_copy(
        src_ref=part_ref.at[OWN, 1 - p], dst_ref=even_ref.at[p, 3], send_sem=back_send, recv_sem=even_sem,
        device_id=(d, across), device_id_type=MESH,
    )
    own_across.start()
    sent.append(own_across)
    pltpu.make_async_copy(part_ref.at[OWN, p], even_ref.at[p, 3], even_sem).start()

    out = dot(rounded, values, first)
    grad_queries = dot(grad_scores, keys, first) * INV
    rows_ref[:, :, 0] = out.astype(jnp.bfloat16).reshape(PAIR, 2, C, D)
    rows_ref[:, :, 1] = grad_queries.astype(jnp.bfloat16).reshape(PAIR, 2, C, D)
    pltpu.make_async_copy(rows_ref.at[b, 0], got_ref.at[b, 0], rows_sem).start()
    for of, which, to in ((1 - b, 0, (d, mate)), (1 - b, 1, (other_core, mate)), (b, 1, (other_core, h))):
        remote = pltpu.make_async_remote_copy(
            src_ref=rows_ref.at[of, which], dst_ref=got_ref.at[b, which], send_sem=rows_send, recv_sem=rows_sem,
            device_id=to, device_id_type=MESH,
        )
        remote.start()
        sent.append(remote)

    sum_sends = []

    def add_up(buffer, sem, start):
        pltpu.make_async_copy(buffer, buffer, sem).wait()
        total = jnp.sum(buffer[...].astype(jnp.float32), axis=(0, 1))
        acc_ref[...] = total if start else acc_ref[...] + total

    pl.when(g == 0)(lambda: pl.semaphore_wait(opposite_sem, 1))
    for turn, place in enumerate((1, 0)):
        pl.when(place == c)(functools.partial(add_up, even_ref, even_sem, True))
        pl.when(place != c)(functools.partial(add_up, odd_ref, odd_sem, True))
        pl.when(place == late)(functools.partial(add_up, recall_ref, recall_sem, False))
        sums_out[h, place] = acc_ref[...].astype(jnp.bfloat16)
        for k, at in enumerate(heads):
            remote = pltpu.make_async_remote_copy(
                src_ref=sums_out.at[h, place], dst_ref=sums_out.at[h, place],
                send_sem=sums_send.at[turn, k], recv_sem=sums_sem.at[turn, k],
                device_id=(d, at), device_id_type=MESH,
            )
            remote.start()
            sum_sends.append(remote)

    pltpu.make_async_copy(got_ref, got_ref, rows_sem).wait()
    for which, place in ((0, c), (1, 1 - c)):
        total = sum(got_ref[n, which].astype(jnp.float32) for n in range(PAIR))
        for n in range(2):
            rows_out[n, place] = total[n].astype(jnp.bfloat16)

    for copy in sent:
        copy.wait_send()
    for at, copy in sent_maybe:
        pl.when(at != d)(copy.wait_send)
    for copy in sum_sends:
        copy.wait_send()
        copy.wait_recv()


def lay_out_kernel(rows_ref, sums_ref, out_ref, dq_ref, dk_ref, dv_ref):
    out_ref[...] = rows_ref[0].reshape(2 * C, D)
    dq_ref[...] = rows_ref[1].reshape(2 * C, D)
    for h in range(HEADS):
        g, q = divmod(h, GROUP)
        for s in range(2):
            rows = slice(s * C + q * QUARTER, s * C + (q + 1) * QUARTER)
            dk_ref[g, rows] = sums_ref[h, s, 0]
            dv_ref[g, rows] = sums_ref[h, s, 1]


def on_device(queries, keys, values, grad_out, episode_lengths, key_stretches):
    vmem = pl.BlockSpec(memory_space=pltpu.VMEM)
    dma = pltpu.SemaphoreType.DMA
    bf16 = jnp.bfloat16
    inputs = [
        pltpu.with_memory_space_constraint(x, pltpu.HBM)
        for x in (queries, keys, values, grad_out, episode_lengths, key_stretches.T)
    ]
    rows, sums = pl.pallas_call(
        attend_kernel,
        out_shape=(
            pltpu.VMEM((2, 2, C, D), bf16),
            pltpu.VMEM((HEADS, 2, 2, QUARTER, D), bf16),
        ),
        in_specs=[pl.BlockSpec(memory_space=pltpu.HBM)] * 6,
        out_specs=(vmem, vmem),
        scratch_shapes=[
            pltpu.VMEM((2, PAIR, 2, C, D), bf16),
            pltpu.VMEM((SLOTS, 2, HALF, D), bf16),
            pltpu.VMEM((SLOTS * HALF, 2 * C), jnp.float32),
            pltpu.VMEM((PAIR, 8, ROWS), jnp.float32),
            pltpu.VMEM((SLOTS, 2, 2, QUARTER, D), bf16),
            pltpu.VMEM((2, 4, 2, QUARTER, D), bf16),
            pltpu.VMEM((2, 5, 2, QUARTER, D), bf16),
            pltpu.VMEM((2, 2, 2, QUARTER, D), bf16),
            pltpu.VMEM((2, QUARTER, D), jnp.float32),
            pltpu.VMEM((PAIR, 2, 2, C, D), bf16),
            pltpu.VMEM((PAIR, 2, 2, C, D), bf16),
            pltpu.SMEM((HEADS,), jnp.int32),
            pltpu.SMEM((4, 2 * PAIRS), jnp.int32),
            dma((2,)), dma, dma, dma, dma, dma, dma, dma, dma((2, HEADS - 1)),
            dma, dma, dma, dma, dma, dma((2, HEADS - 1)), pltpu.SemaphoreType.REGULAR,
        ],
        compiler_params=pltpu.CompilerParams(
            collective_id=0, has_side_effects=True, vmem_limit_bytes=16 * 1024 * 1024
        ),
        name="attend",
    )(*inputs)
    half = jax.ShapeDtypeStruct((2 * C, D), bf16)
    both = jax.ShapeDtypeStruct((2, 2 * C, D), bf16)
    return pl.pallas_call(
        lay_out_kernel,
        out_shape=(half, half, both, both),
        in_specs=[vmem] * 2,
        out_specs=(vmem,) * 4,
        name="lay_out",
    )(*(pltpu.with_memory_space_constraint(x, pltpu.VMEM) for x in (rows, sums)))


def solution(mesh):
    return jax.shard_map(
        on_device,
        mesh=mesh,
        in_specs=(
            P("ctx", "head"),
            P(None, "ctx", None),
            P(None, "ctx", None),
            P("ctx", "head"),
            P(),
            P(),
        ),
        out_specs=(P("ctx", "head"), P("ctx", "head"), P(None, "ctx", None), P(None, "ctx", None)),
        check_vma=False,
    )
```

```python
import functools
import math

import jax
import jax.numpy as jnp
from jax import lax
from jax.experimental import pallas as pl
from jax.experimental.pallas import tpu as pltpu
from jax.sharding import PartitionSpec as P

MESH = pl.DeviceIdType.MESH
C = 64
HALF = 32
QUARTER = 16
HEADS = 8
GROUP = 4
PAIR = 2
PAIRS = 64
ROWS = PAIR * 2 * C
CHIPS = 32
Z_CHIPS = 8
SLOTS = 11
OWN, OTHER, RECALL = 7, 8, 9
D = 128
MASKED = -1e30
EVEN_STEPS = (1, 2, 3)
ODD_STEPS = (1, 2, 3, 4)
INV = 1.0 / math.sqrt(D)


def device_of(pair):
    pair = lax.rem(pair + 2 * PAIRS, PAIRS)
    return jnp.where(pair < PAIRS // 2, 2 * pair, 2 * PAIRS - 1 - 2 * pair)


def attend_kernel(
    q_hbm, k_hbm, v_hbm, do_hbm, ep_hbm, ks_hbm,
    rows_out, sums_out,
    qdo_ref, kv_ref, bias_ref, stat_ref, part_ref, even_ref, odd_ref, recall_ref, acc_ref, rows_ref, got_ref,
    ep_ref, ks_ref,
    in_sems, kv_sem, q_sem, stat_sem, even_sem, odd_sem, recall_sem, rows_sem, sums_sem,
    kv_send, q_send, stat_send, back_send, rows_send, sums_send, opposite_sem,
):
    d = lax.axis_index("ctx")
    h = lax.axis_index("head")
    m, c = d // 2, d % 2
    g, p, b = h // GROUP, h % PAIR, h // PAIR % 2
    mate = h + 2 - 4 * b
    across = h + 1 - 2 * p
    opposite = h + 4 - 8 * g
    mine = jnp.where(c == 0, m, PAIRS - 1 - m)
    other = PAIRS - 1 - mine
    other_core = 2 * m + 1 - c
    far_chip = lax.rem(m + CHIPS // 2, CHIPS)
    late = jnp.where(m >= CHIPS // 2, 1, 0)

    even_to = [device_of(mine + k) for k in EVEN_STEPS]
    even_from = [device_of(mine - k) for k in EVEN_STEPS]
    odd_with = [device_of(other + k) for k in ODD_STEPS]
    far = [2 * far_chip, 2 * far_chip + 1]
    heads = [(1 - g) * GROUP + (h + k) % GROUP for k in (0, 1, 3, 2)] + [g * GROUP + (h + k) % GROUP for k in (2, 1, 3)]

    barrier = pltpu.get_barrier_semaphore()

    def greet(ctx_at, head_at):
        pl.semaphore_signal(barrier, inc=1, device_id=(ctx_at, head_at), device_id_type=MESH)

    for at in odd_with[::-1]:
        pl.when(at != d)(functools.partial(greet, at, h))
    for at in even_from[::-1] + far + [other_core]:
        greet(at, h)
    for at in (mate, across):
        greet(d, at)
    pl.when(g == 0)(functools.partial(greet, d, opposite))
    greet(other_core, mate)

    even_rows, odd_rows = pl.ds(c * C, C), pl.ds((1 - c) * C, C)
    loads = [
        pltpu.make_async_copy(ep_hbm, ep_ref, in_sems.at[0]),
        pltpu.make_async_copy(ks_hbm, ks_ref, in_sems.at[1]),
    ]
    own = [
        pltpu.make_async_copy(q_hbm.at[even_rows], qdo_ref.at[0, b, 0], q_sem),
        pltpu.make_async_copy(do_hbm.at[even_rows], qdo_ref.at[1, b, 0], q_sem),
        pltpu.make_async_copy(k_hbm.at[g, pl.ds(c * C + b * HALF, HALF)], kv_ref.at[OWN, 0], kv_sem),
        pltpu.make_async_copy(v_hbm.at[g, pl.ds(c * C + b * HALF, HALF)], kv_ref.at[OWN, 1], kv_sem),
    ]
    for copy in loads + own:
        copy.start()

    self_count = jnp.where(lax.rem(mine, PAIRS // 2) < 2, 1, 0)
    pl.semaphore_wait(barrier, 4 + 3 + 2 + 1 + 2 + 1 + g - self_count)

    sent, sent_maybe = [], []

    def send_kv(stretch, slot, at, may_be_self=False):
        rows = pl.ds(stretch * C + b * HALF, HALF)
        for which, ref in enumerate((k_hbm, v_hbm)):
            remote = pltpu.make_async_remote_copy(
                src_ref=ref.at[g, rows], dst_ref=kv_ref.at[slot, which], send_sem=kv_send, recv_sem=kv_sem,
                device_id=(at, h), device_id_type=MESH,
            )
            if may_be_self:
                local = pltpu.make_async_copy(ref.at[g, rows], kv_ref.at[slot, which], kv_sem)
                pl.when(at != d)(remote.start)
                pl.when(at == d)(local.start)
                sent_maybe.append((at, remote))
            else:
                remote.start()
                sent.append(remote)

    def send_q(rows, which, to):
        for n, ref in enumerate((q_hbm, do_hbm)):
            remote = pltpu.make_async_remote_copy(
                src_ref=ref.at[rows], dst_ref=qdo_ref.at[n, b, which], send_sem=q_send, recv_sem=q_sem,
                device_id=to, device_id_type=MESH,
            )
            remote.start()
            sent.append(remote)

    for k, at in zip(ODD_STEPS[::-1], odd_with[::-1]):
        send_kv(1 - c, 8 - 2 * k, at, may_be_self=True)
    for k, at in zip(EVEN_STEPS[::-1], even_to[::-1]):
        send_kv(c, 7 - 2 * k, at)
    for at in far:
        send_kv(late, RECALL + c, at)
    send_kv(1 - c, OTHER, other_core)
    send_q(even_rows, 0, (d, mate))
    send_q(odd_rows, 1, (other_core, mate))
    send_q(odd_rows, 1, (other_core, h))

    for copy in loads:
        copy.wait()
    lane = lax.broadcasted_iota(jnp.int32, (1, 2 * C), 1)
    query_pos = 2 * mine * C + lane
    first_pos = jnp.zeros_like(query_pos)
    start = jnp.int32(0)
    for e in range(HEADS - 1):
        start = start + ep_ref[e]
        first_pos = jnp.where(start <= query_pos, start, first_pos)
    row_of = (2 * d + c, 2 * other_core + c)
    entries = [[ks_ref[e, row] for e in range(4)] for row in row_of]
    far_valid = jnp.logical_or(late == 1, c == 1)
    key_row = lax.broadcasted_iota(jnp.int32, (HALF, 2 * C), 0) + b * HALF
    for slot in range(SLOTS):
        if slot < RECALL:
            stretch = 2 * mine - 7 + slot
        else:
            at = far[slot - RECALL]
            stretch = jnp.where(far_valid, jnp.where(late == 1, at, 2 * PAIRS - 1 - at), -1)
        base = []
        for row in entries:
            hit = row[0] == stretch
            for entry in row[1:]:
                hit = jnp.logical_or(hit, entry == stretch)
            base.append(jnp.where(hit, stretch * C, -(1 << 20)))
        key_pos = key_row + jnp.where(lane < C, base[0], base[1])
        seen = (key_pos >= first_pos) & (key_pos <= query_pos)
        bias_ref[pl.ds(slot * HALF, HALF), :] = jnp.where(seen, 0.0, MASKED)

    pltpu.make_async_copy(qdo_ref, qdo_ref, q_sem).wait()
    pltpu.make_async_copy(kv_ref, kv_ref, kv_sem).wait()

    queries = qdo_ref[0].reshape(ROWS, D)
    grads = qdo_ref[1].reshape(ROWS, D)
    keys = kv_ref[:, 0].reshape(SLOTS * HALF, D)
    values = kv_ref[:, 1].reshape(SLOTS * HALF, D)
    last = (((1,), (1,)), ((), ()))
    first = (((0,), (0,)), ((), ()))
    plain = (((1,), (0,)), ((), ()))

    def dot(a, b, dims):
        return lax.dot_general(a, b, dims, preferred_element_type=jnp.float32)

    scores = dot(keys, queries, last) * INV + jnp.concatenate([bias_ref[...]] * PAIR, axis=1)
    top = jnp.max(scores, axis=0, keepdims=True)
    weights = jnp.exp(scores - top)
    mass = jnp.sum(weights, axis=0, keepdims=True)
    grad_weights = dot(values, grads, last)
    inner = jnp.sum(weights * grad_weights, axis=0, keepdims=True)

    stat_ref[b, 0:1] = top
    stat_ref[b, 1:2] = mass
    stat_ref[b, 2:3] = inner
    remote = pltpu.make_async_remote_copy(
        src_ref=stat_ref.at[b], dst_ref=stat_ref.at[b], send_sem=stat_send, recv_sem=stat_sem,
        device_id=(d, mate), device_id_type=MESH,
    )
    remote.start()
    sent.append(remote)
    remote.wait_recv()
    @pl.when(g == 1)
    def _():
        pl.semaphore_signal(opposite_sem, inc=1, device_id=(d, opposite), device_id_type=MESH)

    tops = [stat_ref[n, 0:1] for n in range(PAIR)]
    top_all = functools.reduce(jnp.maximum, tops)
    shares = [jnp.exp(t - top_all) for t in tops]
    mass_all = sum(shares[n] * stat_ref[n, 1:2] for n in range(PAIR))
    inner_all = sum(shares[n] * stat_ref[n, 2:3] for n in range(PAIR))
    over = 1.0 / mass_all
    weights = weights * (jnp.exp(top - top_all) * over)
    rounded = weights.astype(jnp.bfloat16)
    grad_scores = (weights * (grad_weights - inner_all * over)).astype(jnp.bfloat16)
    part_ref[:, :, 0] = (dot(grad_scores, queries, plain) * INV).astype(jnp.bfloat16).reshape(SLOTS, 2, QUARTER, D)
    part_ref[:, :, 1] = dot(rounded, grads, plain).astype(jnp.bfloat16).reshape(SLOTS, 2, QUARTER, D)

    def send_back(slot, buffer, sem, to, at, may_be_self=False):
        far_plane = pltpu.make_async_remote_copy(
            src_ref=part_ref.at[slot, 1 - p], dst_ref=buffer.at[p, to], send_sem=back_send, recv_sem=sem,
            device_id=(at, across), device_id_type=MESH,
        )
        far_plane.start()
        sent.append(far_plane)
        remote = pltpu.make_async_remote_copy(
            src_ref=part_ref.at[slot, p], dst_ref=buffer.at[p, to], send_sem=back_send, recv_sem=sem,
            device_id=(at, h), device_id_type=MESH,
        )
        if may_be_self:
            local = pltpu.make_async_copy(part_ref.at[slot, p], buffer.at[p, to], sem)
            pl.when(at != d)(remote.start)
            pl.when(at == d)(local.start)
            sent_maybe.append((at, remote))
        else:
            remote.start()
            sent.append(remote)

    for n, at in enumerate(far):
        send_back(RECALL + n, recall_ref, recall_sem, c, at)
    for k, at in zip(ODD_STEPS[::-1], odd_with[::-1]):
        send_back(8 - 2 * k, odd_ref, odd_sem, k - 1, at, may_be_self=True)
    for k, at in zip(EVEN_STEPS[::-1], even_from[::-1]):
        send_back(7 - 2 * k, even_ref, even_sem, k - 1, at)
    send_back(OTHER, odd_ref, odd_sem, 4, other_core)
    own_across = pltpu.make_async_remote_copy(
        src_ref=part_ref.at[OWN, 1 - p], dst_ref=even_ref.at[p, 3], send_sem=back_send, recv_sem=even_sem,
        device_id=(d, across), device_id_type=MESH,
    )
    own_across.start()
    sent.append(own_across)
    pltpu.make_async_copy(part_ref.at[OWN, p], even_ref.at[p, 3], even_sem).start()

    out = dot(rounded, values, first)
    grad_queries = dot(grad_scores, keys, first) * INV
    rows_ref[:, :, 0] = out.astype(jnp.bfloat16).reshape(PAIR, 2, C, D)
    rows_ref[:, :, 1] = grad_queries.astype(jnp.bfloat16).reshape(PAIR, 2, C, D)
    pltpu.make_async_copy(rows_ref.at[b, 0], got_ref.at[b, 0], rows_sem).start()
    for of, which, to in ((1 - b, 0, (d, mate)), (1 - b, 1, (other_core, mate)), (b, 1, (other_core, h))):
        remote = pltpu.make_async_remote_copy(
            src_ref=rows_ref.at[of, which], dst_ref=got_ref.at[b, which], send_sem=rows_send, recv_sem=rows_sem,
            device_id=to, device_id_type=MESH,
        )
        remote.start()
        sent.append(remote)

    sum_sends = []

    def add_up(buffer, sem, start):
        pltpu.make_async_copy(buffer, buffer, sem).wait()
        total = jnp.sum(buffer[...].astype(jnp.float32), axis=(0, 1))
        acc_ref[...] = total if start else acc_ref[...] + total

    pl.when(g == 0)(lambda: pl.semaphore_wait(opposite_sem, 1))
    for turn, place in enumerate((1, 0)):
        pl.when(place == c)(functools.partial(add_up, even_ref, even_sem, True))
        pl.when(place != c)(functools.partial(add_up, odd_ref, odd_sem, True))
        pl.when(place == late)(functools.partial(add_up, recall_ref, recall_sem, False))
        sums_out[h, place] = acc_ref[...].astype(jnp.bfloat16)
        for k, at in enumerate(heads):
            remote = pltpu.make_async_remote_copy(
                src_ref=sums_out.at[h, place], dst_ref=sums_out.at[h, place],
                send_sem=sums_send.at[turn, k], recv_sem=sums_sem.at[turn, k],
                device_id=(d, at), device_id_type=MESH,
            )
            remote.start()
            sum_sends.append(remote)

    pltpu.make_async_copy(got_ref, got_ref, rows_sem).wait()
    for which, place in ((0, c), (1, 1 - c)):
        total = sum(got_ref[n, which].astype(jnp.float32) for n in range(PAIR))
        for n in range(2):
            rows_out[n, place] = total[n].astype(jnp.bfloat16)

    for copy in sent:
        copy.wait_send()
    for at, copy in sent_maybe:
        pl.when(at != d)(copy.wait_send)
    for copy in sum_sends:
        copy.wait_send()
        copy.wait_recv()


def lay_out_kernel(rows_ref, sums_ref, out_ref, dq_ref, dk_ref, dv_ref):
    out_ref[...] = rows_ref[0].reshape(2 * C, D)
    dq_ref[...] = rows_ref[1].reshape(2 * C, D)
    for h in range(HEADS):
        g, q = divmod(h, GROUP)
        for s in range(2):
            rows = slice(s * C + q * QUARTER, s * C + (q + 1) * QUARTER)
            dk_ref[g, rows] = sums_ref[h, s, 0]
            dv_ref[g, rows] = sums_ref[h, s, 1]


def on_device(queries, keys, values, grad_out, episode_lengths, key_stretches):
    vmem = pl.BlockSpec(memory_space=pltpu.VMEM)
    dma = pltpu.SemaphoreType.DMA
    bf16 = jnp.bfloat16
    inputs = [
        pltpu.with_memory_space_constraint(x, pltpu.HBM)
        for x in (queries, keys, values, grad_out, episode_lengths, key_stretches.T)
    ]
    rows, sums = pl.pallas_call(
        attend_kernel,
        out_shape=(
            pltpu.VMEM((2, 2, C, D), bf16),
            pltpu.VMEM((HEADS, 2, 2, QUARTER, D), bf16),
        ),
        in_specs=[pl.BlockSpec(memory_space=pltpu.HBM)] * 6,
        out_specs=(vmem, vmem),
        scratch_shapes=[
            pltpu.VMEM((2, PAIR, 2, C, D), bf16),
            pltpu.VMEM((SLOTS, 2, HALF, D), bf16),
            pltpu.VMEM((SLOTS * HALF, 2 * C), jnp.float32),
            pltpu.VMEM((PAIR, 8, ROWS), jnp.float32),
            pltpu.VMEM((SLOTS, 2, 2, QUARTER, D), bf16),
            pltpu.VMEM((2, 4, 2, QUARTER, D), bf16),
            pltpu.VMEM((2, 5, 2, QUARTER, D), bf16),
            pltpu.VMEM((2, 2, 2, QUARTER, D), bf16),
            pltpu.VMEM((2, QUARTER, D), jnp.float32),
            pltpu.VMEM((PAIR, 2, 2, C, D), bf16),
            pltpu.VMEM((PAIR, 2, 2, C, D), bf16),
            pltpu.SMEM((HEADS,), jnp.int32),
            pltpu.SMEM((4, 2 * PAIRS), jnp.int32),
            dma((2,)), dma, dma, dma, dma, dma, dma, dma, dma((2, HEADS - 1)),
            dma, dma, dma, dma, dma, dma((2, HEADS - 1)), pltpu.SemaphoreType.REGULAR,
        ],
        compiler_params=pltpu.CompilerParams(
            collective_id=0, has_side_effects=True, vmem_limit_bytes=16 * 1024 * 1024
        ),
        name="attend",
    )(*inputs)
    half = jax.ShapeDtypeStruct((2 * C, D), bf16)
    both = jax.ShapeDtypeStruct((2, 2 * C, D), bf16)
    return pl.pallas_call(
        lay_out_kernel,
        out_shape=(half, half, both, both),
        in_specs=[vmem] * 2,
        out_specs=(vmem,) * 4,
        name="lay_out",
    )(*(pltpu.with_memory_space_constraint(x, pltpu.VMEM) for x in (rows, sums)))


def solution(mesh):
    return jax.shard_map(
        on_device,
        mesh=mesh,
        in_specs=(
            P("ctx", "head"),
            P(None, "ctx", None),
            P(None, "ctx", None),
            P("ctx", "head"),
            P(),
            P(),
        ),
        out_specs=(P("ctx", "head"), P("ctx", "head"), P(None, "ctx", None), P(None, "ctx", None)),
        check_vma=False,
    )
```
